512 devices in a mesh: ep: 128 (over z, y, core), tp: 4 (over x).
Axes of the slice: x: 4, y: 8, z: 8, core: 2. Of those that a mesh axis runs over, the one named last changes fastest.
Arguments:
- tokens: bfloat16 [2048, 2048], P('ep', 'tp'), may hold values from -6 to 6
- out_grad: bfloat16 [2048, 2048], P('ep', 'tp'), may hold values from -6 to 6
- gate_weights: bfloat16 [2048, 6], P('ep'), may hold values from 0.049804688 to 0.5
- expert_ids: int32 [2048, 6], P('ep'), may hold values from 0 to 63, all different within a row; in each aligned block of 16 rows (0 to 15, 16 to 31, ...) at most 2 rows name the same one
- w_gate: bfloat16 [128, 2048, 512], P('ep', None, 'tp'), may hold values from -0.125 to 0.125
- w_up: bfloat16 [128, 2048, 512], P('ep', None, 'tp'), may hold values from -0.125 to 0.125
- w_down: bfloat16 [128, 512, 2048], P('ep', 'tp'), may hold values from -0.1875 to 0.1875
- shared_gate: bfloat16 [2048, 1408], P('ep', 'tp'), may hold values from -0.125 to 0.125
- shared_up: bfloat16 [2048, 1408], P('ep', 'tp'), may hold values from -0.125 to 0.125
- shared_down: bfloat16 [1408, 2048], P('tp', 'ep'), may hold values from -0.15625 to 0.15625
Outputs:
- grad_tokens: bfloat16 [2048, 2048], P('ep', 'tp')
- grad_gates: float32 [2048, 6], P('ep')
- gate_grad: bfloat16 [128, 2048, 512], P('ep', None, 'tp')
- up_grad: bfloat16 [128, 2048, 512], P('ep', None, 'tp')
- down_grad: bfloat16 [128, 512, 2048], P('ep', 'tp')
The draws below stay inside these ranges and needn't reach their ends.
Inputs may be any that keep to these rules, and one draw needn't show every extreme that they name: `expert_ids`: each row names 6 different experts. In each aligned block of 16 rows (the tokens of one index of ep) no expert is named by more than 2 rows, a bound that some block reaches.
All inputs are finite; a program needn't handle non-finite values.
Results may differ from the reference program's by a relative error of at most 0.015.
Values may be sent and summed in bfloat16 or wider, within the bound.
A program may use at most 64 MiB of HBM per device.

```python
import math
import jax
import jax.numpy as jnp
import numpy as np
from jax import lax

D = 2048
EXPERTS = 64
EH = 1024
SH = 1408
TOPK = 6
TOK_GRP = 16
CAP = 2
TOKENS = 2048
UNITS = 128
UH = 512
N_EP = 128
N_TP = 4


def levels(own_key, dims, cuts, low, largest):
    factor_of = 1.0
    for axis_at, parts in cuts:
        heights = jax.random.uniform(jax.random.fold_in(jax.random.fold_in(own_key, 6), axis_at), (parts,), jnp.float32, low / len(cuts), largest / len(cuts))
        factor_of = factor_of * jnp.repeat(jnp.exp(heights), dims[axis_at] // parts).reshape((-1,) + (1,) * (len(dims) - 1 - axis_at))
    return factor_of


def shared_out(key, own, number, rows, amount, top, reach, slope):
    sequence = jax.random.permutation(key, amount)
    crowded, ordinary = shares(amount, rows * top, reach, slope, True), shares(amount, rows * top, reach, slope, False)
    places = jnp.arange(amount)

    def named(lengths, offset_by):
        used = int((lengths > 0).sum())
        fixed = max(1, used // 4)
        moved = fixed + (places - fixed + offset_by * (used - fixed)) % max(1, amount - fixed)
        return jnp.zeros((amount,), jnp.int32).at[sequence[jnp.where(places < fixed, places, moved)]].set(jnp.asarray(lengths, jnp.int32))

    lengths = jnp.where(number % 4 == 0, named(crowded, number // 4), named(ordinary, number - number // 4 - 1))
    mixed = jax.random.permutation(jax.random.fold_in(own, 3), amount)
    donor, sink = mixed[0:amount // 2 * 2:2], mixed[1:amount // 2 * 2:2]
    margin = jnp.minimum(lengths[donor] - 1, reach - lengths[sink]) // 2
    margin = jnp.where((donor == sequence[0]) | (sink == sequence[0]) | (lengths[sink] == 0), 0, jnp.maximum(margin, 0))
    moved = jax.random.randint(jax.random.fold_in(own, 4), (amount // 2,), 0, 1 << 20) % (margin + 1)
    lengths = lengths.at[donor].add(-moved).at[sink].add(moved)
    labels = jnp.searchsorted(jnp.cumsum(lengths), jnp.arange(rows * top), side="right").astype(jnp.int32)
    listing = labels.reshape(top, rows).T
    listing = listing[jax.random.permutation(jax.random.fold_in(own, 1), rows)]
    offset_by = jax.random.randint(jax.random.fold_in(own, 2), (rows, 1), 0, top)
    return jnp.take_along_axis(listing, (jnp.arange(top)[None, :] + offset_by) % top, axis=1)


def shares(number_of, total, limit, slope, full):
    loads = [(1 << 20) // math.isqrt(grade ** slope) + 1 for grade in range(1, number_of + 1)]
    largest = limit if full else min(limit, max(-(-total // number_of), total * loads[0] // sum(loads)))
    least = 1 if total - largest >= number_of - 1 else 0
    holding, rest = [largest] + [least] * (number_of - 1), total - largest - least * (number_of - 1)
    while rest > 0:
        free = [i for i in range(1, number_of) if holding[i] < largest] or [i for i in range(1, number_of) if holding[i] < limit]
        mass, left = sum([loads[i] for i in free]), rest
        for i in free:
            extra = min(limit - holding[i], max(1, left * loads[i] // mass), rest)
            holding[i] = holding[i] + extra
            rest = rest - extra
    return np.array(holding)


def centred(stream_key, shape, spread, limit, cuts=(), kind=jnp.bfloat16):
    values = spread * jax.random.normal(stream_key, shape, jnp.float32)
    if cuts:
        values = values * levels(stream_key, shape, cuts, -0.22, 0.18)
    return jnp.clip(values, -limit, limit).astype(kind)


def setup_inputs(seed: int = 0) -> dict:
    splits = jax.random.split(jax.random.key(seed), 11)
    tokens = centred(splits[0], (TOKENS, D), 1.0, 6.0, ((0, 128), (1, 4)))
    out_grad = centred(splits[1], (TOKENS, D), 1.0, 6.0, ((0, 128), (1, 4)))
    gate_weights = jnp.clip(0.049804688 + 0.4501953 * jax.random.uniform(splits[2], (TOKENS, TOPK), jnp.float32) ** levels(splits[2], (TOKENS, TOPK), ((0, 128),), -0.2, 0.2), 0.049804688, 0.5).astype(jnp.bfloat16)
    expert_ids_keys = jax.random.split(jax.random.fold_in(splits[3], 1), TOKENS // TOK_GRP)
    expert_ids_turns = jax.random.permutation(jax.random.fold_in(splits[3], 3), TOKENS // TOK_GRP)
    expert_ids = jax.vmap(lambda own, number: shared_out(jax.random.fold_in(splits[3], 2), own, number, TOK_GRP, EXPERTS, TOPK, CAP, 1))(expert_ids_keys, expert_ids_turns).reshape((TOKENS, TOPK))
    w_gate = centred(splits[4], (UNITS, D, UH), D ** -0.5, 0.125, ((0, 128), (2, 4)))
    w_up = centred(splits[5], (UNITS, D, UH), D ** -0.5, 0.125, ((0, 128), (2, 4)))
    w_down = centred(splits[6], (UNITS, UH, D), EH ** -0.5, 0.1875, ((0, 128), (1, 4)))
    shared_gate = centred(splits[7], (D, SH), D ** -0.5, 0.125, ((0, 128), (1, 4)))
    shared_up = centred(splits[8], (D, SH), D ** -0.5, 0.125, ((0, 128), (1, 4)))
    shared_down = centred(splits[9], (SH, D), SH ** -0.5, 0.15625, ((0, 4), (1, 128)))
    return {"tokens": tokens, "out_grad": out_grad, "gate_weights": gate_weights, "expert_ids": expert_ids, "w_gate": w_gate, "w_up": w_up, "w_down": w_down, "shared_gate": shared_gate, "shared_up": shared_up, "shared_down": shared_down}


def silu_parts(pre_gate, pre_up, back_proj, scaling):
    sigma = jax.nn.sigmoid(pre_gate)
    active = pre_gate * sigma
    hidden = active * pre_up
    scaled = scaling * back_proj
    grad_pre_gate = (scaled * pre_up * sigma * (1.0 + pre_gate * (1.0 - sigma))).astype(jnp.bfloat16)
    grad_pre_up = (scaled * active).astype(jnp.bfloat16)
    return hidden, grad_pre_gate, grad_pre_up


def round_trip(values):
    return lax.optimization_barrier(values.astype(jnp.bfloat16)).astype(jnp.float32)


def slot_table(expert_ids):
    ids = expert_ids.reshape(N_EP, TOK_GRP, TOPK)
    hits = (ids[..., None] == jnp.arange(EXPERTS, dtype=jnp.int32)).astype(jnp.int32)
    counts = jnp.sum(hits, axis=2, dtype=jnp.int32)
    before = jnp.cumsum(counts, axis=1, dtype=jnp.int32) - counts
    position = jnp.sum(hits * before[:, :, None, :], axis=3, dtype=jnp.int32)
    groups = jnp.arange(N_EP, dtype=jnp.int32)[:, None, None]
    slots = (ids * (N_EP * CAP) + groups * CAP + position).reshape(-1)
    picks = jnp.arange(TOKENS * TOPK, dtype=jnp.int32)
    table = jnp.full((EXPERTS * N_EP * CAP,), TOKENS * TOPK, dtype=jnp.int32)
    return table.at[slots].set(picks).reshape(EXPERTS, N_EP * CAP)


def reference(tokens, out_grad, gate_weights, expert_ids, w_gate, w_up, w_down, shared_gate, shared_up, shared_down):
    table = slot_table(expert_ids)
    tok_pad = jnp.concatenate([tokens, jnp.zeros((1, D), jnp.bfloat16)], axis=0)
    grad_pad = jnp.concatenate([out_grad, jnp.zeros((1, D), jnp.bfloat16)], axis=0)
    gate_pad = jnp.concatenate([gate_weights.reshape(-1), jnp.zeros((1,), jnp.bfloat16)], axis=0)
    blocks = 2 * N_TP
    block_width = EH // blocks
    rows_all = N_EP * CAP

    def one_expert(carry, expert):
        routed, router = carry
        picks = table[expert]
        rows = picks // TOPK
        tok_rows = tok_pad[rows]
        grad_rows = grad_pad[rows]
        scaling = gate_pad[picks].astype(jnp.float32)[:, None]
        gate_pair = lax.dynamic_slice_in_dim(w_gate, 2 * expert, 2, 0)
        up_pair = lax.dynamic_slice_in_dim(w_up, 2 * expert, 2, 0)
        down_pair = lax.dynamic_slice_in_dim(w_down, 2 * expert, 2, 0)
        gate_mat = jnp.concatenate([gate_pair[0], gate_pair[1]], axis=1)
        up_mat = jnp.concatenate([up_pair[0], up_pair[1]], axis=1)
        down_mat = jnp.concatenate([down_pair[0], down_pair[1]], axis=0)
        pre_gate = jnp.dot(tok_rows, gate_mat, preferred_element_type=jnp.float32)
        pre_up = jnp.dot(tok_rows, up_mat, preferred_element_type=jnp.float32)
        back_proj = lax.dot_general(grad_rows, down_mat, (((1,), (1,)), ((), ())), preferred_element_type=jnp.float32)
        hidden, d_gate, d_up = silu_parts(pre_gate, pre_up, back_proj, scaling)
        router_part = jnp.sum(hidden * back_proj, axis=1)
        weighted = (scaling * hidden).astype(jnp.bfloat16)
        gate_full = jnp.dot(tok_rows.T, d_gate, preferred_element_type=jnp.float32).astype(jnp.bfloat16)
        up_full = jnp.dot(tok_rows.T, d_up, preferred_element_type=jnp.float32).astype(jnp.bfloat16)
        down_full = jnp.dot(weighted.T, grad_rows, preferred_element_type=jnp.float32).astype(jnp.bfloat16)
        dg_blocks = d_gate.astype(jnp.float32).reshape(rows_all, blocks, block_width)
        du_blocks = d_up.astype(jnp.float32).reshape(rows_all, blocks, block_width)
        wg_blocks = gate_mat.astype(jnp.float32).reshape(D, blocks, block_width)
        wu_blocks = up_mat.astype(jnp.float32).reshape(D, blocks, block_width)
        pieces = jnp.einsum("rnb,dnb->nrd", dg_blocks, wg_blocks) + jnp.einsum("rnb,dnb->nrd", du_blocks, wu_blocks)
        contrib = jnp.sum(round_trip(pieces), axis=0)
        routed = routed.at[rows].add(contrib)
        router = router.at[picks].add(router_part)
        gate_units = gate_full.reshape(D, 2, UH).transpose(1, 0, 2)
        up_units = up_full.reshape(D, 2, UH).transpose(1, 0, 2)
        down_units = down_full.reshape(2, UH, D)
        return (routed, router), (gate_units, up_units, down_units)

    start = (jnp.zeros((TOKENS + 1, D), jnp.float32), jnp.zeros((TOKENS * TOPK + 1,), jnp.float32))
    (routed, router), (gate_grad, up_grad, down_grad) = lax.scan(one_expert, start, jnp.arange(EXPERTS, dtype=jnp.int32))

    shared_pre_gate = jnp.dot(tokens, shared_gate, preferred_element_type=jnp.float32)
    shared_pre_up = jnp.dot(tokens, shared_up, preferred_element_type=jnp.float32)
    shared_back = lax.dot_general(out_grad, shared_down, (((1,), (1,)), ((), ())), preferred_element_type=jnp.float32)
    unused, shared_d_gate, shared_d_up = silu_parts(shared_pre_gate, shared_pre_up, shared_back, 1.0)
    shared_width = SH // N_TP
    shared_total = jnp.zeros((TOKENS, D), jnp.float32)
    for block in range(N_TP):
        low = block * shared_width
        high = low + shared_width
        piece = lax.dot_general(shared_d_gate[:, low:high], shared_gate[:, low:high], (((1,), (1,)), ((), ())), preferred_element_type=jnp.float32)
        piece = piece + lax.dot_general(shared_d_up[:, low:high], shared_up[:, low:high], (((1,), (1,)), ((), ())), preferred_element_type=jnp.float32)
        shared_total = shared_total + round_trip(piece)
    grad_tokens = (routed[:TOKENS] + shared_total).astype(jnp.bfloat16)
    grad_gates = router[:TOKENS * TOPK].reshape(TOKENS, TOPK)
    return (grad_tokens, grad_gates, gate_grad.reshape(UNITS, D, UH), up_grad.reshape(UNITS, D, UH), down_grad.reshape(UNITS, UH, D))
```

```python
import functools

import jax
import jax.numpy as jnp
from jax import lax
from jax.experimental import pallas as pl
from jax.experimental.pallas import tpu as pltpu
from jax.sharding import PartitionSpec as P

MESH = pl.DeviceIdType.MESH
BF = jnp.bfloat16
F32 = jnp.float32
NX = 4
LANES = 128
TILES = 9
FIRST = 5


def dot(a, b, ca, cb, **kw):
    return lax.dot_general(a, b, (((ca,), (cb,)), ((), ())), preferred_element_type=F32, **kw)


def iota(shape, dim):
    return lax.broadcasted_iota(jnp.int32, shape, dim)


def one_hot(cond):
    return jnp.where(cond, 1.0, 0.0).astype(BF)


def kernel(
    n,
    tok_ref, dy_ref, gw_ref, ids_ref, wg_hbm, wu_hbm, wd_hbm, sg_ref, su_ref, sd_ref,
    gt_ref, gg_ref, ggrad_hbm, ugrad_hbm, dgrad_hbm,
    pack_a, pack_b, buf_a, buf_b, mid_a, mid_b, end_b, rx, rd,
    wg, wu, wd, ggrad, ugrad, dgrad,
    sib_out, sib_in, rs_out, rs_in, ra_out, rb_out, ra_1, rb_1, ra_mid, rb_mid, ra_2, rb_2,
    sel, s_out, sx, g1, g2, pre_out, pre_in, piece_out, piece_in, fx_out, fx_in,
    ssem, rsem, lsem,
):
    toks, feats = tok_ref.shape
    hid = wg_hbm.shape[2]
    rows = 2 * n * n
    msg = 2 * n
    half = feats // 2
    shared = sg_ref.shape[1]
    la = 3 * feats // 4

    ep = lax.axis_index("ep")
    x = lax.axis_index("tp")
    c = lax.rem(ep, 2)
    y = lax.rem(ep // 2, n)
    z = ep // (2 * n)
    sib = (ep + 1 - 2 * c, x)

    def at_y(k):
        return ((z * n + lax.rem(y + k, n)) * 2 + c, x)

    def at_z(k):
        return ((lax.rem(z + k, n) * n + y) * 2 + c, x)

    def at_x(k):
        return (ep, lax.rem(x + k, NX))

    taken = [0]
    ends = []

    def take(count):
        base = taken[0]
        taken[0] += count
        assert taken[0] <= ssem.shape[0]
        return base

    def copy(src, dst, sem, to):
        return pltpu.make_async_remote_copy(
            src_ref=src, dst_ref=dst, send_sem=ssem.at[sem], recv_sem=rsem.at[sem],
            device_id=to, device_id_type=MESH,
        )

    class Group:
        def __init__(self, count, make):
            self.count, self.make, self.base = count, make, take(count - 1)
            ends.append(self.wait_send)

        def each(self, method):
            def step(k, carry):
                getattr(self.make(k, self.base + k - 1), method)()
                return carry

            lax.fori_loop(1, self.count, step, 0)

        def start(self):
            self.each("start")

        def wait_recv(self):
            self.each("wait_recv")

        def wait_send(self):
            self.each("wait_send")

    def single(src, dst, to):
        made = copy(src, dst, take(1), to)
        ends.append(made.wait_send)
        return made

    loads = [
        pltpu.make_async_copy(a.at[0], b, lsem.at[i])
        for i, (a, b) in enumerate(((wg_hbm, wg), (wu_hbm, wu), (wd_hbm, wd)))
    ]
    for load in loads:
        load.start()

    barrier = pltpu.get_barrier_semaphore()

    def greet(k, carry):
        for to in (at_y(k), at_z(k)):
            pl.semaphore_signal(barrier, inc=1, device_id=to, device_id_type=MESH)
        return carry

    lax.fori_loop(1, n, greet, 0)
    for k in range(NX):
        if k:
            pl.semaphore_signal(barrier, inc=1, device_id=at_x(k), device_id_type=MESH)
        pl.semaphore_signal(
            barrier, inc=1, device_id=(sib[0], lax.rem(x + k, NX)), device_id_type=MESH
        )

    ids = ids_ref[...]
    gates = gw_ref[...].astype(F32)
    lane = iota((toks, rows), 1)
    slot = lane % 2
    outer, inner = lane // msg, (lane // 2) % n
    earlier = one_hot(iota((toks, toks), 0) > iota((toks, toks), 1))

    def place(expert):
        named = [ids[:, k : k + 1] == expert for k in range(ids.shape[1])]
        hits = functools.reduce(jnp.logical_or, named)
        before = dot(earlier, one_hot(hits), 1, 0)
        here = jnp.logical_and(hits, before == slot.astype(F32))
        weight = sum(
            jnp.where(named[k], gates[:, k : k + 1], 0.0) for k in range(len(named))
        )
        return named, here, weight

    named_a, here_a, _ = place(((z + outer) % n) * n + (y + inner) % n)
    _, here_b, weight_b = place(((z + inner) % n) * n + (y + outer) % n)
    place_a = one_hot(here_a)
    place_b = one_hot(here_b)
    put_a = jnp.where(here_a, 1.0, 0.0).T.astype(BF)
    put_b = jnp.where(here_b, weight_b, 0.0).T.astype(BF)
    tok = tok_ref[...]
    dy = dy_ref[...]
    pack_a[...] = dot(put_a, tok, 1, 0).astype(BF).reshape(n, msg, feats)
    pack_b[...] = dot(put_b, dy, 1, 0).astype(BF).reshape(n, msg, feats)

    turned_row = iota((rows, rows), 0)
    turned = ((turned_row // 2) % n) * msg + (turned_row // msg) * 2 + turned_row % 2
    turn = one_hot(iota((rows, rows), 1) == turned)

    col = iota((feats, feats), 1)
    col_in = col % half
    feature = 32 * (col_in // 16) + 16 * (col // half) + col_in % 16
    sel[...] = one_hot(iota((feats, feats), 0) == feature)
    s_all = dot(jnp.concatenate([tok, dy], axis=0), sel[...], 1, 0).astype(BF)
    s_out[0] = s_all[:, :half]
    s_out[1] = s_all[:, half:]

    eye = one_hot(iota((16, 16), 0) == iota((16, 16), 1))
    sd_t = dot(eye, sd_ref[...], 1, 1).astype(BF)
    tiles = []
    for block in (sg_ref[...], su_ref[...], sd_t):
        pad = jnp.zeros((16, TILES // 3 * LANES - shared), BF)
        block = jnp.concatenate([block, pad], axis=1)
        tiles += [block[:, i * LANES : (i + 1) * LANES] for i in range(TILES // 3)]
    for i, tile in enumerate(tiles):
        if i < FIRST:
            g1[y, z, i] = tile
        else:
            g2[z, y, i - FIRST] = tile

    pl.semaphore_wait(barrier, 2 * (n - 1) + 2 * NX - 1)

    a1 = Group(n, lambda k, s: copy(pack_a.at[k], buf_a.at[k], s, at_z(k)))
    b1 = Group(n, lambda k, s: copy(pack_b.at[k], buf_b.at[k], s, at_y(k)))
    a1.start()
    b1.start()
    s_same = Group(NX, lambda k, s: copy(s_out.at[c], sx.at[c, x], s, at_x(k)))
    s_same.start()
    s_other = [
        single(s_out.at[1 - c], sx.at[c, x], (sib[0], lax.rem(x + k, NX))) for k in range(NX)
    ]
    for made in s_other:
        made.start()
    sx[c, x] = s_out[c]
    w1 = Group(n, lambda k, s: copy(g1.at[y, z], g1.at[y, z], s, at_z(k)))
    w2 = Group(n, lambda k, s: copy(g2.at[z, y], g2.at[z, y], s, at_y(k)))
    w1.start()
    w2.start()

    buf_a[0] = pack_a[0]
    buf_b[0] = pack_b[0]

    a1.wait_recv()
    mid_a[...] = dot(turn, buf_a[...].reshape(rows, feats), 1, 0).astype(BF).reshape(n, msg, feats)

    def part(k):
        return pl.ds(pl.multiple_of(k * msg, msg), msg)

    a2 = Group(n, lambda k, s: copy(mid_a.at[k], rx.at[c, x, part(k)], s, at_y(k)))
    a2.start()
    rx[c, x, 0:msg] = mid_a[0]
    b1.wait_recv()
    mid_b[...] = dot(turn, buf_b[...].reshape(rows, feats), 1, 0).astype(BF).reshape(n, msg, feats)
    b2 = Group(n, lambda k, s: copy(mid_b.at[k], end_b.at[k], s, at_z(k)))
    b2.start()
    end_b[0] = mid_b[0]

    class Ring:
        def __init__(self, buf, pos, go):
            self.buf, self.pos, self.go, self.step = buf, pos, go, 0
            self.flying = []

        def block(self, k):
            return lax.rem(self.pos + k + 2 * n, n)

        def forward(self):
            for made in self.flying:
                made.wait_recv()
            s = self.step
            self.flying = []
            if s < n // 2 - 1:
                for way in (1, -1):
                    at = self.buf.at[self.block(-way * s)]
                    self.flying.append(single(at, at, self.go(way % n)))
            elif s == n // 2 - 1:
                for way in (1, -1):
                    span = pl.ds(0, n // 2) if way == 1 else pl.ds(n // 2, n // 2)
                    at = self.buf.at[self.block(-way * s), span]
                    self.flying.append(single(at, at, self.go(way % n)))
            for made in self.flying:
                made.start()
            self.step += 1

    ring1 = Ring(g1, y, at_y)
    ring2 = Ring(g2, z, at_z)
    w1.wait_recv()
    ring1.forward()
    w2.wait_recv()
    ring2.forward()

    a2.wait_recv()
    mine_x = rx.at[c, x]
    x_right = single(mine_x, mine_x, at_x(1))
    x_left = single(mine_x, mine_x, at_x(NX - 1))
    x_sib = Group(NX + 1, lambda k, s: copy(
        rx.at[c, lax.rem(x + k - 1, NX)], rx.at[c, lax.rem(x + k - 1, NX)], s, sib))
    d_sib = Group(NX + 1, lambda k, s: copy(
        rd.at[c, lax.rem(x + k - 1, NX)], rd.at[c, lax.rem(x + k - 1, NX)], s, sib))

    def to_sib(group, k):
        group.make(k + 1, group.base + k).start()

    x_right.start()
    x_left.start()
    to_sib(x_sib, 0)
    b2.wait_recv()
    rd[c, x] = dot(turn, end_b[...].reshape(rows, feats), 1, 0).astype(BF)
    mine_d = rd.at[c, x]
    d_right = single(mine_d, mine_d, at_x(1))
    d_left = single(mine_d, mine_d, at_x(NX - 1))
    d_right.start()
    d_left.start()
    to_sib(d_sib, 0)

    ring1.forward()
    ring2.forward()

    from_left = lax.rem(x + NX - 1, NX)
    from_right = lax.rem(x + 1, NX)
    x_right.wait_recv()
    x_on = single(rx.at[c, from_left], rx.at[c, from_left], at_x(1))
    x_on.start()
    to_sib(x_sib, 3)
    x_left.wait_recv()
    to_sib(x_sib, 1)
    d_left.wait_recv()
    d_on = single(rd.at[c, from_right], rd.at[c, from_right], at_x(NX - 1))
    d_on.start()
    to_sib(d_sib, 1)
    d_right.wait_recv()
    to_sib(d_sib, 3)

    ring1.forward()
    ring2.forward()

    x_on.wait_recv()
    to_sib(x_sib, 2)
    d_on.wait_recv()
    to_sib(d_sib, 2)

    ring1.forward()
    ring2.forward()

    for load in loads:
        load.wait()
    x_sib.wait_recv()
    d_sib.wait_recv()

    def quarter(ref, q):
        return jnp.concatenate([ref[0, q], ref[1, q]], axis=0)

    def w_quarter(q):
        span = slice(q * feats, (q + 1) * feats)
        return jnp.concatenate([wg[span], wu[span]], axis=1)

    pre = sum(dot(quarter(rx, q), w_quarter(q), 1, 0) for q in range(NX))
    q_back = sum(
        dot(quarter(rd, q), wd[:, q * feats : (q + 1) * feats], 1, 1) for q in range(NX)
    )

    def silu_parts(pre_gate, pre_up, back):
        sigma = jax.nn.sigmoid(pre_gate)
        active = pre_gate * sigma
        d_gate = back * pre_up * sigma * (1.0 + pre_gate * (1.0 - sigma))
        return active * pre_up, jnp.concatenate([d_gate, back * active], axis=1).astype(BF)

    hidden, d_both = silu_parts(pre[:, :hid], pre[:, hid:], q_back)
    router = jnp.sum(hidden * q_back, axis=1, keepdims=True)
    hidden = hidden.astype(BF)

    def coded(value):
        first = value.astype(BF).astype(F32)
        at = iota((value.shape[0], LANES), 1)
        return jnp.where(at == 0, first, jnp.where(at == 1, value - first, 0.0)).astype(BF)

    first_half = c == 0
    d_own = jnp.where(first_half, d_both[:rows], d_both[rows:])
    d_sibs = jnp.where(first_half, d_both[rows:], d_both[:rows])
    r_own = jnp.where(first_half, router[:rows], router[rows:])
    r_sibs = jnp.where(first_half, router[rows:], router[:rows])

    for q in range(NX):
        sib_out[:, q * feats : (q + 1) * feats] = dot(d_sibs, w_quarter(q), 1, 1).astype(BF)
    sib_out[:, NX * feats :] = coded(r_sibs)
    part_sib = single(sib_out, sib_in, sib)
    part_sib.start()
    own = [dot(d_own, w_quarter(q), 1, 1) for q in range(NX)]
    part_sib.wait_recv()
    r_chip = r_own + jnp.sum(sib_in[:, NX * feats :].astype(F32), axis=1, keepdims=True)
    r_coded = coded(r_chip)
    for q in range(NX):
        total = own[q] + sib_in[:, q * feats : (q + 1) * feats].astype(F32)
        rs_out[q, :, :feats] = total.astype(BF)
        rs_out[q, :, feats:] = r_coded
    rs = Group(NX, lambda k, s: copy(
        rs_out.at[lax.rem(x + k, NX)], rs_in.at[k], s, at_x(k)))
    rs.start()

    stores = []
    for i, (a, b) in enumerate(((ggrad, ggrad_hbm), (ugrad, ugrad_hbm), (dgrad, dgrad_hbm))):
        stores.append(pltpu.make_async_copy(a, b.at[0], lsem.at[3 + i]))
    for q in range(NX):
        span = slice(q * feats, (q + 1) * feats)
        both = dot(quarter(rx, q), d_both, 0, 0).astype(BF)
        ggrad[span] = both[:, :hid]
        ugrad[span] = both[:, hid:]
        dgrad[:, span] = dot(hidden, quarter(rd, q), 0, 0).astype(BF)
    for store in stores:
        store.start()

    rs.wait_recv()
    summed = rs_out[x].astype(F32)
    for k in range(1, NX):
        summed = summed + rs_in[k].astype(F32)
    r_total = coded(jnp.sum(summed[:, feats:], axis=1, keepdims=True))
    ra_out[...] = summed[:, :la].astype(BF).reshape(n, msg, la)
    rest = jnp.concatenate([summed[:, la:feats].astype(BF), r_total], axis=1)
    lb = rest.shape[1]
    rb_out[...] = dot(turn, rest, 1, 0).astype(BF).reshape(n, msg, lb)
    back_a1 = Group(n, lambda k, s: copy(ra_out.at[k], ra_1.at[k], s, at_y(n - k)))
    back_b1 = Group(n, lambda k, s: copy(rb_out.at[k], rb_1.at[k], s, at_z(n - k)))
    back_a1.start()
    back_b1.start()
    ra_1[0] = ra_out[0]
    rb_1[0] = rb_out[0]

    ring1.forward()
    ring2.forward()
    s_same.wait_recv()
    for made in s_other:
        made.wait_recv()

    def weights(i):
        if i < FIRST:
            parts = [g1[:, k, i].reshape(n * 16, LANES) for k in range(n)]
        else:
            parts = [g2[k, :, i - FIRST].reshape(n * 16, LANES) for k in range(n)]
        return jnp.concatenate(parts, axis=0)

    def matrix(m):
        return jnp.concatenate([weights(3 * m + i) for i in range(3)], axis=1)

    def features(low):
        return jnp.concatenate(
            [
                jnp.concatenate([sx[s, q, low : low + toks] for q in range(NX)], axis=1)
                for s in range(2)
            ],
            axis=0,
        )

    width = 3 * LANES
    s_tok = features(0)
    s_dy = features(toks)
    pre_out[:, :width] = dot(s_tok, matrix(0), 1, 0)
    pre_out[:, width : 2 * width] = dot(s_tok, matrix(1), 1, 0)
    pre_out[:, 2 * width :] = dot(s_dy, matrix(2), 1, 0)
    pre_sib = single(pre_out, pre_in, sib)
    pre_sib.start()

    back_a1.wait_recv()
    ra_mid[...] = dot(turn, ra_1[...].reshape(rows, la), 1, 0).astype(BF).reshape(n, msg, la)
    back_a2 = Group(n, lambda k, s: copy(ra_mid.at[k], ra_2.at[k], s, at_z(n - k)))
    back_a2.start()
    ra_2[0] = ra_mid[0]
    back_b1.wait_recv()
    rb_mid[...] = dot(turn, rb_1[...].reshape(rows, lb), 1, 0).astype(BF).reshape(n, msg, lb)
    back_b2 = Group(n, lambda k, s: copy(rb_mid.at[k], rb_2.at[k], s, at_y(n - k)))
    back_b2.start()
    rb_2[0] = rb_mid[0]

    pre_sib.wait_recv()
    s_pre = pre_out[...] + pre_in[...]
    _, s_both = silu_parts(s_pre[:, :width], s_pre[:, width : 2 * width], s_pre[:, 2 * width :])
    piece = dot(s_both[:, :width], matrix(0), 1, 1) + dot(s_both[:, width:], matrix(1), 1, 1)
    for q in range(NX):
        piece_out[q] = piece[:, q * half : (q + 1) * half].astype(BF)
    s_rs = Group(NX, lambda k, s: copy(
        piece_out.at[lax.rem(x + k, NX)], piece_in.at[k], s, at_x(k)))
    s_rs.start()
    s_rs.wait_recv()
    s_sum = piece_out[x].astype(F32)
    for k in range(1, NX):
        s_sum = s_sum + piece_in[k].astype(F32)
    s_sum = s_sum.astype(BF)
    s_own = jnp.where(first_half, s_sum[:toks], s_sum[toks:])
    fx_out[...] = jnp.where(first_half, s_sum[toks:], s_sum[:toks])
    s_fx = single(fx_out, fx_in, sib)
    s_fx.start()

    back_a2.wait_recv()
    back_b2.wait_recv()
    ret_b = rb_2[...].reshape(rows, lb)
    routed = jnp.concatenate(
        [
            dot(place_a, ra_2[...].reshape(rows, la), 1, 0),
            dot(place_b, ret_b[:, : feats - la], 1, 0),
        ],
        axis=1,
    )
    expert_b = ((z + inner) % n) * n + (y + outer) % n
    picked = jnp.concatenate(
        [
            one_hot(jnp.logical_and(here_b, ids[:, k : k + 1] == expert_b))
            for k in range(ids.shape[1])
        ],
        axis=0,
    )
    routers = jnp.sum(dot(picked, ret_b[:, feats - la :], 1, 0), axis=1, keepdims=True)
    gg_ref[...] = jnp.concatenate(
        [routers[k * toks : (k + 1) * toks] for k in range(ids.shape[1])], axis=1
    ) / gates
    s_fx.wait_recv()
    s_other_half = fx_in[...]
    both_halves = jnp.concatenate(
        [
            jnp.where(first_half, s_own, s_other_half),
            jnp.where(first_half, s_other_half, s_own),
        ],
        axis=1,
    )
    gt_ref[...] = (routed + dot(both_halves, sel[...], 1, 1)).astype(BF)

    for store in stores:
        store.wait()
    for end in ends:
        end()


def body(tokens, out_grad, gate_weights, expert_ids, w_gate, w_up, w_down, s_gate, s_up, s_down):
    n = round((lax.axis_size("ep") // 2) ** 0.5)
    toks, feats = tokens.shape
    hid = w_gate.shape[2]
    rows, msg, half = 2 * n * n, 2 * n, feats // 2
    la = 3 * feats // 4
    lb = feats + LANES - la
    vmem = pl.BlockSpec(memory_space=pltpu.VMEM)
    hbm = pl.BlockSpec(memory_space=pl.ANY)

    def legs(lanes, count):
        return [pltpu.VMEM((n, msg, lanes), BF) for _ in range(count)]

    def like(a):
        return jax.ShapeDtypeStruct(a.shape, a.dtype)

    scratch = (
        legs(feats, 7)
        + [pltpu.VMEM((2, NX, rows, feats), BF)] * 2
        + [pltpu.VMEM(a.shape[1:], BF) for a in (w_gate, w_up, w_down)] * 2
        + [pltpu.VMEM((rows, NX * feats + LANES), BF)] * 2
        + [pltpu.VMEM((NX, rows, feats + LANES), BF)] * 2
        + legs(la, 1) + legs(lb, 1) + legs(la, 1) + legs(lb, 1)
        + legs(la, 1) + legs(lb, 1) + legs(la, 1) + legs(lb, 1)
        + [
            pltpu.VMEM((feats, feats), BF),
            pltpu.VMEM((2, 2 * toks, half), BF),
            pltpu.VMEM((2, NX, 2 * toks, half), BF),
            pltpu.VMEM((n, n, FIRST, 16, LANES), BF),
            pltpu.VMEM((n, n, TILES - FIRST, 16, LANES), BF),
            pltpu.VMEM((2 * toks, TILES * LANES), F32),
            pltpu.VMEM((2 * toks, TILES * LANES), F32),
            pltpu.VMEM((NX, 2 * toks, half), BF),
            pltpu.VMEM((NX, 2 * toks, half), BF),
            pltpu.VMEM((toks, half), BF),
            pltpu.VMEM((toks, half), BF),
            pltpu.SemaphoreType.DMA((140,)),
            pltpu.SemaphoreType.DMA((140,)),
            pltpu.SemaphoreType.DMA((6,)),
        ]
    )
    return pl.pallas_call(
        functools.partial(kernel, n),
        out_shape=(
            like(tokens),
            jax.ShapeDtypeStruct(gate_weights.shape, F32),
            like(w_gate),
            like(w_up),
            like(w_down),
        ),
        in_specs=[vmem] * 4 + [hbm] * 3 + [vmem] * 3,
        out_specs=(vmem, vmem, hbm, hbm, hbm),
        scratch_shapes=scratch,
        compiler_params=pltpu.CompilerParams(
            collective_id=0, has_side_effects=True, vmem_limit_bytes=48 * 1024 * 1024
        ),
    )(tokens, out_grad, gate_weights, expert_ids, w_gate, w_up, w_down, s_gate, s_up, s_down)


def solution(mesh):
    placed = (
        P("ep", "tp"),
        P("ep", "tp"),
        P("ep", None),
        P("ep", None),
        P("ep", None, "tp"),
        P("ep", None, "tp"),
        P("ep", "tp", None),
        P("ep", "tp"),
        P("ep", "tp"),
        P("tp", "ep"),
    )
    return jax.shard_map(
        body,
        mesh=mesh,
        in_specs=placed,
        out_specs=(
            P("ep", "tp"),
            P("ep", None),
            P("ep", None, "tp"),
            P("ep", None, "tp"),
            P("ep", "tp", None),
        ),
        check_vma=False,
    )
```

```python
import functools
import math

import jax
import jax.numpy as jnp
from jax import lax
from jax.experimental import pallas as pl
from jax.experimental.pallas import tpu as pltpu
from jax.sharding import PartitionSpec as P

MESH = pl.DeviceIdType.MESH
BF = jnp.bfloat16
F32 = jnp.float32
NX = 4
LIMIT = 60 * 1024 * 1024
LANES = 128
TILES = 9
FIRST = 5


def dot(a, b, ca, cb, **kw):
    return lax.dot_general(a, b, (((ca,), (cb,)), ((), ())), preferred_element_type=F32, **kw)


def iota(shape, dim):
    return lax.broadcasted_iota(jnp.int32, shape, dim)


def one_hot(cond):
    return jnp.where(cond, 1.0, 0.0).astype(BF)


def kernel(
    n,
    tok_hbm, dy_hbm, gw_hbm, ids_hbm, wg_hbm, wu_hbm, wd_hbm, sg_hbm, su_hbm, sd_hbm,
    gt_hbm, gg_hbm, ggrad_hbm, ugrad_hbm, dgrad_hbm,
    gt_ref, gg_ref, ggrad, ugrad, dgrad, tok_ref, dy_ref, gw_ref, ids_ref, sg_ref, su_ref, sd_ref,
    pack_a, pack_b, buf_a, buf_b, mid_a, mid_b, rx, rd, wg, wu, wd,
    sib_out, sib_in, rs_out, rs_in, rt_out, rt_in, rr_out, rr_in, ret_out, ret_1, ret_mid, ret_2,
    sel, s_out, sx, g1, g2, pre_out, pre_in, piece_out, piece_in, fx_out, fx_in, tally,
    ssem, rsem, lsem,
):
    toks, feats = tok_ref.shape
    hid = wg_hbm.shape[2]
    rows = 2 * n * n
    msg = 2 * n
    half = feats // 2
    shared = sg_ref.shape[1]
    top = ids_ref.shape[0]
    edges = sorted({0, min(3, n), min(5, n), n})
    chunks = list(zip(edges, edges[1:]))

    ep = lax.axis_index("ep")
    x = lax.axis_index("tp")
    c = lax.rem(ep, 2)
    y = lax.rem(ep // 2, n)
    z = ep // (2 * n)
    sib = (ep + 1 - 2 * c, x)

    def away(p):
        return (p % 2) * ((p + 1) // 2) + (1 - p % 2) * ((n - p // 2) % n)

    def at_y(k):
        return ((z * n + lax.rem(y + k, n)) * 2 + c, x)

    def at_z(k):
        return ((lax.rem(z + k, n) * n + y) * 2 + c, x)

    def at_x(k):
        return (ep, lax.rem(x + k, NX))

    pending = []
    taken = [0]
    sent = [0]

    class Arrival:
        def __init__(self, ref):
            self.ref, self.sem = ref, taken[0]
            taken[0] += 1
            assert self.sem < rsem.shape[0]

        def wait(self):
            pltpu.make_async_copy(self.ref, self.ref, rsem.at[self.sem]).wait()
            pending.remove(self)

    class Local:
        def __init__(self, src, dst, sem):
            self.made = pltpu.make_async_copy(src, dst, lsem.at[sem])

        def start(self):
            self.made.start()
            pending.append(self)

        def wait(self):
            self.made.wait()
            pending.remove(self)

    def size(ref):
        return math.prod(ref.shape) * ref.dtype.itemsize

    def send(src, dst, arrival, to, times=1):
        pltpu.make_async_remote_copy(
            src_ref=src, dst_ref=dst, send_sem=ssem.at[0], recv_sem=rsem.at[arrival.sem],
            device_id=to, device_id_type=MESH,
        ).start()
        sent[0] += times * size(src)
        if arrival not in pending:
            pending.append(arrival)

    def send_each(low, high, arrival, make):
        if low < high:

            def step(p, carry):
                src, dst, to = make(p)
                send(src, dst, arrival, to, high - low)
                return carry

            lax.fori_loop(low, high, step, 0)

    def finish():
        for one in list(pending):
            one.wait()
        span = tally.at[pl.ds(0, sent[0] // 256)]
        pltpu.make_async_copy(span, span, ssem.at[0]).wait()

    barrier = pltpu.get_barrier_semaphore()

    def greet(k, carry):
        for to in (at_y(k), at_z(k)):
            pl.semaphore_signal(barrier, inc=1, device_id=to, device_id_type=MESH)
        return carry

    lax.fori_loop(1, n, greet, 0)
    for k in range(NX):
        if k:
            pl.semaphore_signal(barrier, inc=1, device_id=at_x(k), device_id_type=MESH)
        pl.semaphore_signal(
            barrier, inc=1, device_id=(sib[0], lax.rem(x + k, NX)), device_id_type=MESH
        )

    moves = (
        (ids_hbm, ids_ref), (gw_hbm, gw_ref), (tok_hbm, tok_ref), (dy_hbm, dy_ref),
        (sg_hbm, sg_ref), (su_hbm, su_ref), (sd_hbm, sd_ref),
        (wg_hbm.at[0], wg), (wu_hbm.at[0], wu), (wd_hbm.at[0], wd),
    )
    loads = [Local(a, b, i) for i, (a, b) in enumerate(moves)]
    for load in loads:
        load.start()
    for load in loads[:4]:
        load.wait()

    ids = ids_ref[...]
    gates = gw_ref[...].astype(F32)
    row = iota((rows, toks), 0)
    slot = row % 2
    outer, inner = away(row // msg), away((row // 2) % n)
    earlier = one_hot(iota((toks, toks), 0) < iota((toks, toks), 1))

    def place(expert):
        named = [ids[k : k + 1] == expert for k in range(top)]
        hits = functools.reduce(jnp.logical_or, named)
        before = dot(one_hot(hits), earlier, 1, 0)
        return named, jnp.logical_and(hits, before == slot.astype(F32))

    named_a, here_a = place(((z + outer) % n) * n + (y + inner) % n)
    named_b, here_b = place(((z + inner) % n) * n + (y + outer) % n)
    weight_b = sum(jnp.where(named_b[k], gates[k : k + 1], 0.0) for k in range(top))
    put_a = one_hot(here_a)
    put_b = jnp.where(here_b, weight_b, 0.0).astype(BF)
    tok = tok_ref[...]
    dy = dy_ref[...]
    pack_a[...] = dot(put_a, tok, 1, 0).astype(BF).reshape(n, msg, feats)
    pack_b[...] = dot(put_b, dy, 1, 0).astype(BF).reshape(n, msg, feats)

    pl.semaphore_wait(barrier, 2 * (n - 1) + 2 * NX - 1)

    others = pl.ds(1, n - 1)
    a1 = Arrival(buf_a.at[others])
    b1 = Arrival(buf_b.at[others])
    send_each(1, n, a1, lambda p: (pack_a.at[p], buf_a.at[p], at_z(away(p))))
    send_each(1, n, b1, lambda p: (pack_b.at[p], buf_b.at[p], at_y(away(p))))

    for load in loads[4:7]:
        load.wait()
    tiles = []
    for block in (sg_ref[...], su_ref[...], sd_ref[...]):
        pad = jnp.zeros((16, TILES // 3 * LANES - shared), BF)
        block = jnp.concatenate([block, pad], axis=1)
        tiles += [block[:, i * LANES : (i + 1) * LANES] for i in range(TILES // 3)]
    for i, tile in enumerate(tiles):
        if i < FIRST:
            g1[y, z, i] = tile
        else:
            g2[z, y, i - FIRST] = tile
    w1 = Arrival(g1.at[0, pl.ds(0, n - 1)])
    w2 = Arrival(g2.at[0, pl.ds(0, n - 1)])

    def send_weights():
        send_each(1, n, w1, lambda p: (g1.at[y, z], g1.at[y, z], at_z(away(p))))
        send_each(1, n, w2, lambda p: (g2.at[z, y], g2.at[z, y], at_y(away(p))))

    send_weights()

    col = iota((feats, feats), 1)
    col_in = col % half
    feature = 32 * (col_in // 16) + 16 * (col // half) + col_in % 16
    sel[...] = one_hot(iota((feats, feats), 0) == feature)
    s_all = dot(jnp.concatenate([tok, dy], axis=0), sel[...], 1, 0).astype(BF)
    s_out[0] = s_all[:, :half]
    s_out[1] = s_all[:, half:]
    sx[c, x] = s_out[c]
    s_same = Arrival(sx.at[0, pl.ds(0, NX - 1)])
    s_other = Arrival(sx.at[0])
    send_each(1, NX, s_same, lambda k: (s_out.at[c], sx.at[c, x], at_x(k)))
    send_each(0, NX, s_other, lambda k: (
        s_out.at[1 - c], sx.at[c, x], (sib[0], lax.rem(x + k, NX))))

    turned_row = iota((rows, rows), 0)
    turned = ((turned_row // 2) % n) * msg + (turned_row // msg) * 2 + turned_row % 2
    turn_f32 = jnp.where(iota((rows, rows), 1) == turned, 1.0, 0.0)
    turn = turn_f32.astype(BF)
    buf_a[0] = pack_a[0]
    buf_b[0] = pack_b[0]

    def part(p):
        return pl.ds(pl.multiple_of(p * msg, msg), msg)

    spans = [pl.ds(low * msg, (high - low) * msg) for low, high in chunks]
    a1.wait()
    mid_a[...] = dot(turn, buf_a[...].reshape(rows, feats), 1, 0).astype(BF).reshape(n, msg, feats)
    a2 = [Arrival(mid_a.at[pl.ds(max(low, 1), high - max(low, 1))]) for low, high in chunks]
    for (low, high), arrival in zip(chunks, a2):
        send_each(max(low, 1), high, arrival, lambda p: (
            mid_a.at[p], rx.at[c, x, part(p)], at_y(away(p))))
    rx[c, x, 0:msg] = mid_a[0]
    b1.wait()
    mid_b[...] = dot(turn, buf_b[...].reshape(rows, feats), 1, 0).astype(BF).reshape(n, msg, feats)
    b2 = [Arrival(mid_b.at[pl.ds(max(low, 1), high - max(low, 1))]) for low, high in chunks]
    for (low, high), arrival in zip(chunks, b2):
        send_each(max(low, 1), high, arrival, lambda p: (
            mid_b.at[p], rd.at[c, x, part(p)], at_z(away(p))))
    rd[c, x, 0:msg] = mid_b[0]

    class Ring:
        def __init__(self, buf, pos, go):
            self.buf, self.pos, self.go, self.step = buf, pos, go, 0
            self.flying = []

        def block(self, k):
            return lax.rem(self.pos + k + 2 * n, n)

        def forward(self):
            for arrival in self.flying:
                arrival.wait()
            self.flying = []
            s, last = self.step, n // 2 - 1
            if s <= last:
                if s < last:
                    arrival = Arrival(self.buf.at[pl.ds(0, 2)])
                else:
                    arrival = Arrival(self.buf.at[0])
                self.flying.append(arrival)
                for way in (1, -1):
                    at = self.buf.at[self.block(-way * s)]
                    if s == last:
                        at = at.at[pl.ds(0, n // 2) if way == 1 else pl.ds(n // 2, n // 2)]
                    send(at, at, arrival, self.go(way % n))
            self.step += 1

    ring1 = Ring(g1, y, at_y)
    ring2 = Ring(g2, z, at_z)

    def rings():
        ring1.forward()
        ring2.forward()

    def rings_first():
        w1.wait()
        ring1.forward()
        w2.wait()
        ring2.forward()

    left, right = lax.rem(x + NX - 1, NX), lax.rem(x + 1, NX)
    two = pl.ds(0, 2)
    sib_rows = [Arrival(rx.at[0, two]) for _ in range(NX)]

    def to_x(buf, at, h, k):
        ref = buf.at[c, at, spans[h]]
        arrival = Arrival(ref)
        send(ref, ref, arrival, at_x(k % NX))
        return arrival

    def to_sib(buf, k, h):
        ref = buf.at[c, lax.rem(x + k, NX), spans[h]]
        send(ref, ref, sib_rows[k], sib)

    x_right, x_left, d_right, d_left = [], [], [], []
    for h in range(len(chunks)):
        a2[h].wait()
        x_right.append(to_x(rx, x, h, 1))
        x_left.append(to_x(rx, x, h, -1))
        to_sib(rx, 0, h)
        b2[h].wait()
        d_left.append(to_x(rd, x, h, -1))
        d_right.append(to_x(rd, x, h, 1))
        to_sib(rd, 0, h)
        if h == 1:
            rings_first()

    x_on, d_on = [], []
    for h in range(len(chunks)):
        x_right[h].wait()
        x_on.append(to_x(rx, left, h, 1))
        to_sib(rx, 3, h)
        d_left[h].wait()
        d_on.append(to_x(rd, right, h, -1))
        to_sib(rd, 1, h)
        x_left[h].wait()
        to_sib(rx, 1, h)
        d_right[h].wait()
        to_sib(rd, 3, h)
    rings()

    for load in loads[7:]:
        load.wait()

    def quarter(ref, q):
        return jnp.concatenate([ref[0, q], ref[1, q]], axis=0)

    def at_quarter(q):
        return pl.ds(pl.multiple_of(q * feats, feats), feats)

    def w_quarter(q):
        return jnp.concatenate([wg[at_quarter(q)], wu[at_quarter(q)]], axis=1)

    pre = jnp.zeros((2 * rows, 2 * hid), F32)
    q_back = jnp.zeros((2 * rows, hid), F32)
    for k in (0, 1, 3, 2):
        if k == 2:
            for h in range(len(chunks)):
                x_on[h].wait()
                to_sib(rx, 2, h)
                d_on[h].wait()
                to_sib(rd, 2, h)
        sib_rows[k].wait()
        q = lax.rem(x + k, NX)
        pre = pre + dot(quarter(rx, q), w_quarter(q), 1, 0)
        q_back = q_back + dot(quarter(rd, q), wd[:, at_quarter(q)], 1, 1)

    def both_halves(f, a):
        return jnp.concatenate([f(a[:rows]), f(a[rows:])], axis=0)

    q_back = both_halves(
        lambda a: dot(turn_f32, a, 1, 0, precision=lax.Precision.HIGHEST), q_back
    )

    def silu_parts(pre_gate, pre_up, back):
        sigma = jax.nn.sigmoid(pre_gate)
        active = pre_gate * sigma
        d_gate = back * pre_up * sigma * (1.0 + pre_gate * (1.0 - sigma))
        return active * pre_up, jnp.concatenate([d_gate, back * active], axis=1).astype(BF)

    hidden, d_both = silu_parts(pre[:, :hid], pre[:, hid:], q_back)
    router = jnp.sum(hidden * q_back, axis=1, keepdims=True)
    hidden = both_halves(lambda a: dot(turn, a, 1, 0).astype(BF), hidden.astype(BF))

    first_half = c == 0
    d_own = jnp.where(first_half, d_both[:rows], d_both[rows:])
    d_sibs = jnp.where(first_half, d_both[rows:], d_both[:rows])
    r_own = jnp.where(first_half, router[:rows], router[rows:])
    r_sibs = jnp.where(first_half, router[rows:], router[:rows])

    def coded(value, at):
        first = value.astype(BF).astype(F32)
        return jnp.where(at == 0, first, jnp.where(at == 1, value - first, 0.0)).astype(BF)

    def as_row(column):
        return jnp.broadcast_to(column, (rows, 16)).T

    def row_sum(tile):
        return jnp.sum(tile.astype(F32), axis=0, keepdims=True)

    tile_row = iota((16, rows), 0)
    rt_out[...] = coded(as_row(r_sibs), tile_row)
    router_sib = Arrival(rt_in)
    send(rt_out, rt_in, router_sib, sib)
    part_sib = []
    for k in range(NX):
        sib_out[k] = dot(d_sibs, w_quarter(lax.rem(x + k, NX)), 1, 1).astype(BF)
        part_sib.append(Arrival(sib_in.at[k]))
        send(sib_out.at[k], sib_in.at[k], part_sib[k], sib)
    own = [dot(d_own, w_quarter(lax.rem(x + k, NX)), 1, 1) for k in range(NX)]
    router_sib.wait()
    r_chip = as_row(r_own) + row_sum(rt_in[...])
    rr_out[...] = coded(r_chip, tile_row)
    router_rs = Arrival(rr_in.at[pl.ds(1, NX - 1)])
    send_each(1, NX, router_rs, lambda k: (rr_out, rr_in.at[k], at_x(k)))
    for k in range(NX):
        part_sib[k].wait()
        rs_out[k] = (own[k] + sib_in[k].astype(F32)).astype(BF)
    rs = {}
    for h in reversed(range(len(chunks))):
        rs[h] = Arrival(rs_in.at[pl.ds(1, NX - 1), spans[h]])
        for k in (2, 1, 3):
            send(rs_out.at[k, spans[h]], rs_in.at[k, spans[h]], rs[h], at_x(k))
    rings()

    for q in range(NX):
        span = slice(q * feats, (q + 1) * feats)
        both = dot(quarter(rx, q), d_both, 0, 0).astype(BF)
        ggrad[0, span] = both[:, :hid]
        ugrad[0, span] = both[:, hid:]
        dgrad[0, :, span] = dot(hidden, quarter(rd, q), 0, 0).astype(BF)
    stores = [
        Local(a, b, len(loads) + i)
        for i, (a, b) in enumerate((
            (gt_ref, gt_hbm), (gg_ref, gg_hbm),
            (ggrad, ggrad_hbm), (ugrad, ugrad_hbm), (dgrad, dgrad_hbm),
        ))
    ]
    for store in stores[2:]:
        store.start()

    router_rs.wait()
    r_all = row_sum(rr_out[...])
    for k in range(1, NX):
        r_all = r_all + row_sum(rr_in[k])
    r_total = coded(jnp.broadcast_to(r_all, (LANES, rows)).T, iota((rows, LANES), 1))
    back_1 = Arrival(ret_1.at[others])
    for h in reversed(range(len(chunks))):
        low, high = chunks[h]
        rs[h].wait()
        total = rs_out[0, spans[h]].astype(F32)
        for k in range(1, NX):
            total = total + rs_in[k, spans[h]].astype(F32)
        r_part = r_total[low * msg : high * msg]
        block = jnp.concatenate([total.astype(BF), r_part], axis=1)
        ret_out[low:high] = block.reshape(high - low, msg, feats + LANES)
        send_each(max(low, 1), high, back_1, lambda p: (
            ret_out.at[p], ret_1.at[p], at_y(n - away(p))))
    ret_1[0] = ret_out[0]
    rings()

    def weights(i):
        if i < FIRST:
            parts = [g1[:, k, i].reshape(n * 16, LANES) for k in range(n)]
        else:
            parts = [g2[k, :, i - FIRST].reshape(n * 16, LANES) for k in range(n)]
        return jnp.concatenate(parts, axis=0)

    def matrix(m):
        return jnp.concatenate([weights(3 * m + i) for i in range(3)], axis=1)

    def features(low):
        return jnp.concatenate(
            [
                jnp.concatenate([sx[s, q, low : low + toks] for q in range(NX)], axis=1)
                for s in range(2)
            ],
            axis=0,
        )

    width = 3 * LANES

    def shared_one():
        s_same.wait()
        s_other.wait()
        s_tok = features(0)
        pre_out[:, :width] = dot(s_tok, matrix(0), 1, 0)
        pre_out[:, width : 2 * width] = dot(s_tok, matrix(1), 1, 0)
        pre_out[:, 2 * width :] = dot(features(toks), matrix(2), 1, 0)
        arrival = Arrival(pre_in)
        send(pre_out, pre_in, arrival, sib)
        return arrival


    back_1.wait()
    wide = feats + LANES
    ret_mid[...] = dot(turn, ret_1[...].reshape(rows, wide), 1, 0).astype(BF).reshape(n, msg, wide)
    back_2 = Arrival(ret_2.at[others])
    send_each(1, n, back_2, lambda p: (ret_mid.at[p], ret_2.at[p], at_z(n - away(p))))
    ret_2[0] = ret_mid[0]
    rings()
    pre_sib = shared_one()

    pre_sib.wait()
    s_pre = pre_out[...] + pre_in[...]
    _, s_both = silu_parts(s_pre[:, :width], s_pre[:, width : 2 * width], s_pre[:, 2 * width :])
    piece = dot(s_both[:, :width], matrix(0), 1, 1) + dot(s_both[:, width:], matrix(1), 1, 1)
    for q in range(NX):
        piece_out[q] = piece[:, q * half : (q + 1) * half].astype(BF)
    s_rs = Arrival(piece_in.at[pl.ds(1, NX - 1)])
    send_each(1, NX, s_rs, lambda k: (
        piece_out.at[lax.rem(x + k, NX)], piece_in.at[k], at_x(k)))
    s_rs.wait()
    s_sum = piece_out[x].astype(F32)
    for k in range(1, NX):
        s_sum = s_sum + piece_in[k].astype(F32)
    s_sum = s_sum.astype(BF)
    s_own = jnp.where(first_half, s_sum[:toks], s_sum[toks:])
    fx_out[...] = jnp.where(first_half, s_sum[toks:], s_sum[:toks])
    s_fx = Arrival(fx_in)
    send(fx_out, fx_in, s_fx, sib)

    back_2.wait()
    came = ret_2[...].reshape(rows, wide)
    routed = dot(put_a, came[:, :feats], 0, 0)
    routers = jnp.sum(came[:, feats:].astype(F32), axis=1, keepdims=True)
    gg_ref[...] = jnp.concatenate(
        [
            jnp.sum(
                jnp.where(jnp.logical_and(here_a, named_a[k]), routers, 0.0),
                axis=0, keepdims=True,
            )
            for k in range(top)
        ],
        axis=0,
    ) / gates
    stores[1].start()
    s_fx.wait()
    s_other_half = fx_in[...]
    both = jnp.concatenate(
        [
            jnp.where(first_half, s_own, s_other_half),
            jnp.where(first_half, s_other_half, s_own),
        ],
        axis=1,
    )
    gt_ref[...] = (routed + dot(both, sel[...], 1, 1)).astype(BF)
    stores[0].start()
    finish()


def hand_out(*refs):
    count = (len(refs) - 2) // 3
    ins, outs, held = refs[:count], refs[count : 2 * count], refs[2 * count : 3 * count]
    fetch, store = refs[3 * count :]
    reads = [pltpu.make_async_copy(ins[i], held[i], fetch.at[i]) for i in range(count)]
    writes = [pltpu.make_async_copy(held[i], outs[i], store.at[i]) for i in range(count)]
    for read in reads:
        read.start()
    for read, write in zip(reads, writes):
        read.wait()
        write.start()
    for write in writes:
        write.wait()


def body(tokens, out_grad, gate_weights, expert_ids, w_gate, w_up, w_down, s_gate, s_up, s_down):
    n = round((lax.axis_size("ep") // 2) ** 0.5)
    toks, feats = tokens.shape
    hid = w_gate.shape[2]
    rows, msg, half = 2 * n * n, 2 * n, feats // 2
    vmem = pl.BlockSpec(memory_space=pltpu.VMEM)
    hbm = pl.BlockSpec(memory_space=pltpu.HBM)

    def legs(lanes, count):
        return [pltpu.VMEM((n, msg, lanes), BF) for _ in range(count)]

    def like(a):
        return jax.ShapeDtypeStruct(a.shape, a.dtype)

    arrays = (
        tokens, out_grad, gate_weights.T, expert_ids.T, w_gate, w_up, w_down,
        s_gate, s_up, s_down.T,
    )
    results = (
        like(tokens),
        jax.ShapeDtypeStruct(gate_weights.shape[::-1], F32),
        like(w_gate),
        like(w_up),
        like(w_down),
    )
    scratch = (
        [pltpu.VMEM(a.shape, a.dtype) for a in results]
        + [pltpu.VMEM(arrays[i].shape, arrays[i].dtype) for i in (0, 1, 2, 3, 7, 8, 9)]
        + legs(feats, 6)
        + [pltpu.VMEM((2, NX, rows, feats), BF)] * 2
        + [pltpu.VMEM(a.shape[1:], BF) for a in (w_gate, w_up, w_down)]
        + [pltpu.VMEM((NX, rows, feats), BF)] * 4
        + [pltpu.VMEM((16, rows), BF)] * 3
        + [pltpu.VMEM((NX, 16, rows), BF)]
        + legs(feats + LANES, 4)
        + [
            pltpu.VMEM((feats, feats), BF),
            pltpu.VMEM((2, 2 * toks, half), BF),
            pltpu.VMEM((2, NX, 2 * toks, half), BF),
            pltpu.VMEM((n, n, FIRST, 16, LANES), BF),
            pltpu.VMEM((n, n, TILES - FIRST, 16, LANES), BF),
            pltpu.VMEM((2 * toks, TILES * LANES), F32),
            pltpu.VMEM((2 * toks, TILES * LANES), F32),
            pltpu.VMEM((NX, 2 * toks, half), BF),
            pltpu.VMEM((NX, 2 * toks, half), BF),
            pltpu.VMEM((toks, half), BF),
            pltpu.VMEM((toks, half), BF),
            pltpu.VMEM((32768, LANES), BF),
            pltpu.SemaphoreType.DMA((1,)),
            pltpu.SemaphoreType.DMA((76,)),
            pltpu.SemaphoreType.DMA((len(arrays) + len(results),)),
        ]
    )
    made = pl.pallas_call(
        functools.partial(kernel, n),
        out_shape=results,
        in_specs=[hbm] * len(arrays),
        out_specs=(hbm,) * len(results),
        scratch_shapes=scratch,
        compiler_params=pltpu.CompilerParams(
            collective_id=0, has_side_effects=True, vmem_limit_bytes=LIMIT
        ),
    )(*arrays)
    given = pl.pallas_call(
        hand_out,
        out_shape=results,
        in_specs=[hbm] * len(results),
        out_specs=(hbm,) * len(results),
        scratch_shapes=[pltpu.VMEM(a.shape, a.dtype) for a in results]
        + [pltpu.SemaphoreType.DMA((len(results),))] * 2,
        compiler_params=pltpu.CompilerParams(vmem_limit_bytes=LIMIT),
    )(*made)
    return (given[0], given[1].T) + tuple(given[2:])


def solution(mesh):
    placed = (
        P("ep", "tp"),
        P("ep", "tp"),
        P("ep", None),
        P("ep", None),
        P("ep", None, "tp"),
        P("ep", None, "tp"),
        P("ep", "tp", None),
        P("ep", "tp"),
        P("ep", "tp"),
        P("tp", "ep"),
    )
    return jax.shard_map(
        body,
        mesh=mesh,
        in_specs=placed,
        out_specs=(
            P("ep", "tp"),
            P("ep", None),
            P("ep", None, "tp"),
            P("ep", None, "tp"),
            P("ep", "tp", None),
        ),
        check_vma=False,
    )
```

```python
import functools
import math

import jax
import jax.numpy as jnp
from jax import lax
from jax.experimental import pallas as pl
from jax.experimental.pallas import tpu as pltpu
from jax.sharding import PartitionSpec as P

MESH = pl.DeviceIdType.MESH
BF = jnp.bfloat16
F32 = jnp.float32
NX = 4
LIMIT = 60 * 1024 * 1024
LANES = 128
TILES = 9
FIRST = 5


def dot(a, b, ca, cb, **kw):
    return lax.dot_general(a, b, (((ca,), (cb,)), ((), ())), preferred_element_type=F32, **kw)


def iota(shape, dim):
    return lax.broadcasted_iota(jnp.int32, shape, dim)


def one_hot(cond):
    return jnp.where(cond, 1.0, 0.0).astype(BF)


def kernel(
    n,
    tok_hbm, dy_hbm, gw_hbm, ids_hbm, wg_hbm, wu_hbm, wd_hbm, sg_hbm, su_hbm, sd_hbm,
    gt_hbm, gg_hbm, ggrad_hbm, ugrad_hbm, dgrad_hbm,
    gt_ref, gg_ref, ggrad, ugrad, dgrad, tok_ref, dy_ref, gw_ref, ids_ref, sg_ref, su_ref, sd_ref,
    pack_a, pack_b, buf_a, buf_b, mid_a, mid_b, rx, rd, wg, wu, wd,
    rs_out, rs_in, rr_out, rr_in, dd_out, dd, ret_out, ret_1, ret_mid, ret_2,
    sel, s_out, sx, g1, g2, pre_out, pre_in, piece_out, piece_in, fx_out, fx_in, tally,
    ssem, rsem, lsem,
):
    toks, feats = tok_ref.shape
    hid = wg_hbm.shape[2]
    rows = 2 * n * n
    msg = 2 * n
    half = feats // 2
    shared = sg_ref.shape[1]
    top = ids_ref.shape[0]
    edges = sorted({0, min(3, n), min(5, n), n})
    chunks = list(zip(edges, edges[1:]))

    ep = lax.axis_index("ep")
    x = lax.axis_index("tp")
    c = lax.rem(ep, 2)
    y = lax.rem(ep // 2, n)
    z = ep // (2 * n)
    sib = (ep + 1 - 2 * c, x)

    def away(p):
        return (p % 2) * ((p + 1) // 2) + (1 - p % 2) * ((n - p // 2) % n)

    def at_y(k):
        return ((z * n + lax.rem(y + k, n)) * 2 + c, x)

    def at_z(k):
        return ((lax.rem(z + k, n) * n + y) * 2 + c, x)

    def at_x(k):
        return (ep, lax.rem(x + k, NX))

    pending = []
    taken = [0]
    sent = [0]

    class Arrival:
        def __init__(self, ref):
            self.ref, self.sem = ref, taken[0]
            taken[0] += 1
            assert self.sem < rsem.shape[0]

        def wait(self):
            pltpu.make_async_copy(self.ref, self.ref, rsem.at[self.sem]).wait()
            pending.remove(self)

    class Local:
        def __init__(self, src, dst, sem):
            self.made = pltpu.make_async_copy(src, dst, lsem.at[sem])

        def start(self):
            self.made.start()
            pending.append(self)

        def wait(self):
            self.made.wait()
            pending.remove(self)

    def size(ref):
        return math.prod(ref.shape) * ref.dtype.itemsize

    def send(src, dst, arrival, to, times=1):
        pltpu.make_async_remote_copy(
            src_ref=src, dst_ref=dst, send_sem=ssem.at[0], recv_sem=rsem.at[arrival.sem],
            device_id=to, device_id_type=MESH,
        ).start()
        sent[0] += times * size(src)
        if arrival not in pending:
            pending.append(arrival)

    def send_each(low, high, arrival, make):
        if low < high:

            def step(i, carry):
                src, dst, to = make(low + high - 1 - i)
                send(src, dst, arrival, to, high - low)
                return carry

            lax.fori_loop(low, high, step, 0)

    def finish():
        for one in list(pending):
            one.wait()
        span = tally.at[pl.ds(0, sent[0] // 256)]
        pltpu.make_async_copy(span, span, ssem.at[0]).wait()

    barrier = pltpu.get_barrier_semaphore()

    def greet(k, carry):
        for to in (at_y(k), at_z(k)):
            pl.semaphore_signal(barrier, inc=1, device_id=to, device_id_type=MESH)
        return carry

    lax.fori_loop(1, n, greet, 0)
    for k in range(NX):
        if k:
            pl.semaphore_signal(barrier, inc=1, device_id=at_x(k), device_id_type=MESH)
        pl.semaphore_signal(
            barrier, inc=1, device_id=(sib[0], lax.rem(x + k, NX)), device_id_type=MESH
        )

    moves = (
        (ids_hbm, ids_ref), (gw_hbm, gw_ref), (tok_hbm, tok_ref), (dy_hbm, dy_ref),
        (sg_hbm, sg_ref), (su_hbm, su_ref), (sd_hbm, sd_ref),
        (wg_hbm.at[0], wg.at[c]), (wu_hbm.at[0], wu.at[c]), (wd_hbm.at[0], wd.at[c]),
    )
    loads = [Local(a, b, i) for i, (a, b) in enumerate(moves)]
    for load in loads:
        load.start()
    for load in loads[:4]:
        load.wait()

    ids = ids_ref[...]
    gates = gw_ref[...].astype(F32)
    row = iota((rows, toks), 0)
    slot = row % 2
    outer, inner = away(row // msg), away((row // 2) % n)
    earlier = one_hot(iota((toks, toks), 0) < iota((toks, toks), 1))

    def place(expert):
        named = [ids[k : k + 1] == expert for k in range(top)]
        hits = functools.reduce(jnp.logical_or, named)
        before = dot(one_hot(hits), earlier, 1, 0)
        return named, jnp.logical_and(hits, before == slot.astype(F32))

    named_a, here_a = place(((z + outer) % n) * n + (y + inner) % n)
    named_b, here_b = place(((z + inner) % n) * n + (y + outer) % n)
    weight_b = sum(jnp.where(named_b[k], gates[k : k + 1], 0.0) for k in range(top))
    put_a = one_hot(here_a)
    put_b = jnp.where(here_b, weight_b, 0.0).astype(BF)
    tok = tok_ref[...]
    dy = dy_ref[...]
    pack_a[...] = dot(put_a, tok, 1, 0).astype(BF).reshape(n, msg, feats)
    pack_b[...] = dot(put_b, dy, 1, 0).astype(BF).reshape(n, msg, feats)

    pl.semaphore_wait(barrier, 2 * (n - 1) + 2 * NX - 1)

    others = pl.ds(1, n - 1)
    a1 = Arrival(buf_a.at[others])
    b1 = Arrival(buf_b.at[others])
    send_each(1, n, a1, lambda p: (pack_a.at[p], buf_a.at[p], at_z(away(p))))
    send_each(1, n, b1, lambda p: (pack_b.at[p], buf_b.at[p], at_y(away(p))))

    for load in loads[4:7]:
        load.wait()
    tiles = []
    for block in (sg_ref[...], su_ref[...], sd_ref[...]):
        pad = jnp.zeros((16, TILES // 3 * LANES - shared), BF)
        block = jnp.concatenate([block, pad], axis=1)
        tiles += [block[:, i * LANES : (i + 1) * LANES] for i in range(TILES // 3)]
    for i, tile in enumerate(tiles):
        if i < FIRST:
            g1[y, z, i] = tile
        else:
            g2[z, y, i - FIRST] = tile
    w1 = Arrival(g1.at[0, pl.ds(0, n - 1)])
    w2 = Arrival(g2.at[0, pl.ds(0, n - 1)])

    def send_weights():
        send_each(1, n, w1, lambda p: (g1.at[y, z], g1.at[y, z], at_z(away(p))))
        send_each(1, n, w2, lambda p: (g2.at[z, y], g2.at[z, y], at_y(away(p))))

    send_weights()

    col = iota((feats, feats), 1)
    col_in = col % half
    feature = 32 * (col_in // 16) + 16 * (col // half) + col_in % 16
    sel[...] = one_hot(iota((feats, feats), 0) == feature)
    s_all = dot(jnp.concatenate([tok, dy], axis=0), sel[...], 1, 0).astype(BF)
    s_out[0] = s_all[:, :half]
    s_out[1] = s_all[:, half:]
    sx[c, x] = s_out[c]
    s_same = Arrival(sx.at[0, pl.ds(0, NX - 1)])
    s_other = Arrival(sx.at[0])
    send_each(1, NX, s_same, lambda k: (s_out.at[c], sx.at[c, x], at_x(k)))
    send_each(0, NX, s_other, lambda k: (
        s_out.at[1 - c], sx.at[c, x], (sib[0], lax.rem(x + k, NX))))

    w_sib = []
    for load, ref in zip(loads[7:], (wg, wu, wd)):
        load.wait()
        w_sib.append(Arrival(ref.at[0]))
        send(ref.at[c], ref.at[c], w_sib[-1], sib)

    turned_row = iota((rows, rows), 0)
    turned = ((turned_row // 2) % n) * msg + (turned_row // msg) * 2 + turned_row % 2
    turn_f32 = jnp.where(iota((rows, rows), 1) == turned, 1.0, 0.0)
    turn = turn_f32.astype(BF)
    buf_a[0] = pack_a[0]
    buf_b[0] = pack_b[0]

    def part(p):
        return pl.ds(pl.multiple_of(p * msg, msg), msg)

    spans = [pl.ds(low * msg, (high - low) * msg) for low, high in chunks]
    a1.wait()
    mid_a[...] = dot(turn, buf_a[...].reshape(rows, feats), 1, 0).astype(BF).reshape(n, msg, feats)
    a2 = [Arrival(mid_a.at[pl.ds(max(low, 1), high - max(low, 1))]) for low, high in chunks]
    for (low, high), arrival in zip(chunks, a2):
        send_each(max(low, 1), high, arrival, lambda p: (
            mid_a.at[p], rx.at[c, x, part(p)], at_y(away(p))))
    rx[c, x, 0:msg] = mid_a[0]
    b1.wait()
    mid_b[...] = dot(turn, buf_b[...].reshape(rows, feats), 1, 0).astype(BF).reshape(n, msg, feats)
    b2 = [Arrival(mid_b.at[pl.ds(max(low, 1), high - max(low, 1))]) for low, high in chunks]
    for (low, high), arrival in zip(chunks, b2):
        send_each(max(low, 1), high, arrival, lambda p: (
            mid_b.at[p], rd.at[c, x, part(p)], at_z(away(p))))
    rd[c, x, 0:msg] = mid_b[0]

    class Ring:
        def __init__(self, buf, pos, go):
            self.buf, self.pos, self.go, self.step = buf, pos, go, 0
            self.flying = []

        def block(self, k):
            return lax.rem(self.pos + k + 2 * n, n)

        def forward(self):
            for arrival in self.flying:
                arrival.wait()
            self.flying = []
            s, last = self.step, n // 2 - 1
            if s <= last:
                if s < last:
                    arrival = Arrival(self.buf.at[pl.ds(0, 2)])
                else:
                    arrival = Arrival(self.buf.at[0])
                self.flying.append(arrival)
                for way in (1, -1):
                    at = self.buf.at[self.block(-way * s)]
                    if s == last:
                        at = at.at[pl.ds(0, n // 2) if way == 1 else pl.ds(n // 2, n // 2)]
                    send(at, at, arrival, self.go(way % n))
            self.step += 1

    ring1 = Ring(g1, y, at_y)
    ring2 = Ring(g2, z, at_z)

    def rings():
        ring1.forward()
        ring2.forward()

    def rings_first():
        w1.wait()
        ring1.forward()
        w2.wait()
        ring2.forward()

    left, right = lax.rem(x + NX - 1, NX), lax.rem(x + 1, NX)

    def to_x(buf, at, h, k):
        ref = buf.at[c, at, spans[h]]
        arrival = Arrival(ref)
        send(ref, ref, arrival, at_x(k % NX))
        return arrival

    x_right, x_left, d_right, d_left = [], [], [], []
    for h in range(len(chunks)):
        a2[h].wait()
        x_right.append(to_x(rx, x, h, 1))
        b2[h].wait()
        d_left.append(to_x(rd, x, h, -1))
        x_left.append(to_x(rx, x, h, -1))
        d_right.append(to_x(rd, x, h, 1))
        if h == 1:
            rings_first()

    x_on, d_on = [], []
    for h in range(len(chunks)):
        x_right[h].wait()
        x_on.append(to_x(rx, left, h, 1))
        d_left[h].wait()
        d_on.append(to_x(rd, right, h, -1))
    rings()

    for arrival in w_sib:
        arrival.wait()

    def at_quarter(q):
        return pl.ds(pl.multiple_of(q * feats, feats), feats)

    def w_quarter(q):
        return jnp.concatenate(
            [ref[u, at_quarter(q)] for ref in (wg, wu) for u in range(2)], axis=1
        )

    def down_quarter(q):
        return jnp.concatenate([wd[u, :, at_quarter(q)] for u in range(2)], axis=0)

    both = 2 * hid
    pre = jnp.zeros((rows, 2 * both), F32)
    q_back = jnp.zeros((rows, both), F32)
    for k in (0, 1, 3, 2):
        if k == 1:
            for arrival in x_left:
                arrival.wait()
        if k == 3:
            for arrival in d_right:
                arrival.wait()
        if k == 2:
            for arrival in x_on + d_on:
                arrival.wait()
        q = lax.rem(x + k, NX)
        pre = pre + dot(rx[c, q], w_quarter(q), 1, 0)
        q_back = q_back + dot(rd[c, q], down_quarter(q), 1, 1)
    q_back = dot(turn_f32, q_back, 1, 0, precision=lax.Precision.HIGHEST)

    def silu_parts(pre_gate, pre_up, back):
        sigma = jax.nn.sigmoid(pre_gate)
        active = pre_gate * sigma
        d_gate = back * pre_up * sigma * (1.0 + pre_gate * (1.0 - sigma))
        return active * pre_up, jnp.concatenate([d_gate, back * active], axis=1).astype(BF)

    hidden, d_both = silu_parts(pre[:, :both], pre[:, both:], q_back)
    router = jnp.sum(hidden * q_back, axis=1, keepdims=True)

    def coded(value, at):
        first = value.astype(BF).astype(F32)
        return jnp.where(at == 0, first, jnp.where(at == 1, value - first, 0.0)).astype(BF)

    def as_row(column):
        return jnp.broadcast_to(column, (rows, 16)).T

    def row_sum(tile):
        return jnp.sum(tile.astype(F32), axis=0, keepdims=True)

    tile_row = iota((16, rows), 0)
    rr_out[...] = coded(as_row(router), tile_row)
    router_rs = Arrival(rr_in.at[pl.ds(1, NX - 1)])
    send_each(1, NX, router_rs, lambda k: (rr_out, rr_in.at[k], at_x(k)))
    for k in (2, 1, 3, 0):
        rs_out[k] = dot(d_both, w_quarter(lax.rem(x + k, NX)), 1, 1).astype(BF)
    rs = {}
    for h in reversed(range(len(chunks))):
        rs[h] = Arrival(rs_in.at[pl.ds(1, NX - 1), spans[h]])
        for k in (2, 1, 3):
            send(rs_out.at[k, spans[h]], rs_in.at[k, spans[h]], rs[h], at_x(k))
    rings()

    first_half = c == 0
    hidden = dot(turn, hidden.astype(BF), 1, 0).astype(BF)
    parts = [
        jnp.concatenate(
            [a[:, u * hid : (u + 1) * hid] for a in (d_both[:, :both], d_both[:, both:], hidden)],
            axis=1,
        )
        for u in range(2)
    ]
    dd[c] = jnp.where(first_half, parts[0], parts[1])
    dd_out[...] = jnp.where(first_half, parts[1], parts[0])
    dd_sib, x_sib, d_sib = Arrival(dd.at[0]), Arrival(rx.at[0]), Arrival(rd.at[0])
    send(dd_out, dd.at[c], dd_sib, sib)
    send(rx.at[c], rx.at[c], x_sib, sib)
    send(rd.at[c], rd.at[c], d_sib, sib)
    stores = [
        Local(a, b, len(loads) + i)
        for i, (a, b) in enumerate((
            (gt_ref, gt_hbm), (gg_ref, gg_hbm),
            (ggrad, ggrad_hbm), (ugrad, ugrad_hbm), (dgrad, dgrad_hbm),
        ))
    ]

    def weight_gradients():
        for arrival in (dd_sib, x_sib, d_sib):
            arrival.wait()
        parts = jnp.concatenate([dd[0], dd[1]], axis=0)
        for q in range(NX):
            span = slice(q * feats, (q + 1) * feats)
            rows_x = jnp.concatenate([rx[0, q], rx[1, q]], axis=0)
            rows_d = jnp.concatenate([rd[0, q], rd[1, q]], axis=0)
            grads = dot(rows_x, parts[:, : 2 * hid], 0, 0).astype(BF)
            ggrad[0, span] = grads[:, :hid]
            ugrad[0, span] = grads[:, hid:]
            dgrad[0, :, span] = dot(parts[:, 2 * hid :], rows_d, 0, 0).astype(BF)
        for store in stores[2:]:
            store.start()


    router_rs.wait()
    r_all = row_sum(rr_out[...])
    for k in range(1, NX):
        r_all = r_all + row_sum(rr_in[k])
    r_total = coded(jnp.broadcast_to(r_all, (LANES, rows)).T, iota((rows, LANES), 1))
    back_1 = Arrival(ret_1.at[others])
    for h in reversed(range(len(chunks))):
        low, high = chunks[h]
        rs[h].wait()
        total = rs_out[0, spans[h]].astype(F32)
        for k in range(1, NX):
            total = total + rs_in[k, spans[h]].astype(F32)
        r_part = r_total[low * msg : high * msg]
        block = jnp.concatenate([total.astype(BF), r_part], axis=1)
        ret_out[low:high] = block.reshape(high - low, msg, feats + LANES)
        send_each(max(low, 1), high, back_1, lambda p: (
            ret_out.at[p], ret_1.at[p], at_y(n - away(p))))
    ret_1[0] = ret_out[0]
    weight_gradients()
    rings()

    def weights(i):
        if i < FIRST:
            parts = [g1[:, k, i].reshape(n * 16, LANES) for k in range(n)]
        else:
            parts = [g2[k, :, i - FIRST].reshape(n * 16, LANES) for k in range(n)]
        return jnp.concatenate(parts, axis=0)

    def matrix(m):
        return jnp.concatenate([weights(3 * m + i) for i in range(3)], axis=1)

    def features(low):
        return jnp.concatenate(
            [
                jnp.concatenate([sx[s, q, low : low + toks] for q in range(NX)], axis=1)
                for s in range(2)
            ],
            axis=0,
        )

    width = 3 * LANES

    def shared_one():
        s_same.wait()
        s_other.wait()
        s_tok = features(0)
        pre_out[:, :width] = dot(s_tok, matrix(0), 1, 0)
        pre_out[:, width : 2 * width] = dot(s_tok, matrix(1), 1, 0)
        pre_out[:, 2 * width :] = dot(features(toks), matrix(2), 1, 0)
        arrival = Arrival(pre_in)
        send(pre_out, pre_in, arrival, sib)
        return arrival


    back_1.wait()
    wide = feats + LANES
    ret_mid[...] = dot(turn, ret_1[...].reshape(rows, wide), 1, 0).astype(BF).reshape(n, msg, wide)
    back_2 = Arrival(ret_2.at[others])
    send_each(1, n, back_2, lambda p: (ret_mid.at[p], ret_2.at[p], at_z(n - away(p))))
    ret_2[0] = ret_mid[0]
    rings()
    pre_sib = shared_one()

    pre_sib.wait()
    s_pre = pre_out[...] + pre_in[...]
    _, s_both = silu_parts(s_pre[:, :width], s_pre[:, width : 2 * width], s_pre[:, 2 * width :])
    piece = dot(s_both[:, :width], matrix(0), 1, 1) + dot(s_both[:, width:], matrix(1), 1, 1)
    for q in range(NX):
        piece_out[q] = piece[:, q * half : (q + 1) * half].astype(BF)
    s_rs = Arrival(piece_in.at[pl.ds(1, NX - 1)])
    send_each(1, NX, s_rs, lambda k: (
        piece_out.at[lax.rem(x + k, NX)], piece_in.at[k], at_x(k)))
    s_rs.wait()
    s_sum = piece_out[x].astype(F32)
    for k in range(1, NX):
        s_sum = s_sum + piece_in[k].astype(F32)
    s_sum = s_sum.astype(BF)
    s_own = jnp.where(first_half, s_sum[:toks], s_sum[toks:])
    fx_out[...] = jnp.where(first_half, s_sum[toks:], s_sum[:toks])
    s_fx = Arrival(fx_in)
    send(fx_out, fx_in, s_fx, sib)

    back_2.wait()
    came = ret_2[...].reshape(rows, wide)
    routed = dot(put_a, came[:, :feats], 0, 0)
    routers = jnp.sum(came[:, feats:].astype(F32), axis=1, keepdims=True)
    gg_ref[...] = jnp.concatenate(
        [
            jnp.sum(
                jnp.where(jnp.logical_and(here_a, named_a[k]), routers, 0.0),
                axis=0, keepdims=True,
            )
            for k in range(top)
        ],
        axis=0,
    ) / gates
    stores[1].start()
    s_fx.wait()
    s_other_half = fx_in[...]
    s_both = jnp.concatenate(
        [
            jnp.where(first_half, s_own, s_other_half),
            jnp.where(first_half, s_other_half, s_own),
        ],
        axis=1,
    )
    gt_ref[...] = (routed + dot(s_both, sel[...], 1, 1)).astype(BF)
    stores[0].start()
    finish()


def hand_out(*refs):
    count = (len(refs) - 2) // 3
    ins, outs, held = refs[:count], refs[count : 2 * count], refs[2 * count : 3 * count]
    fetch, store = refs[3 * count :]
    reads = [pltpu.make_async_copy(ins[i], held[i], fetch.at[i]) for i in range(count)]
    writes = [pltpu.make_async_copy(held[i], outs[i], store.at[i]) for i in range(count)]
    for read in reads:
        read.start()
    for read, write in zip(reads, writes):
        read.wait()
        write.start()
    for write in writes:
        write.wait()


def body(tokens, out_grad, gate_weights, expert_ids, w_gate, w_up, w_down, s_gate, s_up, s_down):
    n = round((lax.axis_size("ep") // 2) ** 0.5)
    toks, feats = tokens.shape
    hid = w_gate.shape[2]
    rows, msg, half = 2 * n * n, 2 * n, feats // 2
    vmem = pl.BlockSpec(memory_space=pltpu.VMEM)
    hbm = pl.BlockSpec(memory_space=pltpu.HBM)

    def legs(lanes, count):
        return [pltpu.VMEM((n, msg, lanes), BF) for _ in range(count)]

    def like(a):
        return jax.ShapeDtypeStruct(a.shape, a.dtype)

    arrays = (
        tokens, out_grad, gate_weights.T, expert_ids.T, w_gate, w_up, w_down,
        s_gate, s_up, s_down.T,
    )
    results = (
        like(tokens),
        jax.ShapeDtypeStruct(gate_weights.shape[::-1], F32),
        like(w_gate),
        like(w_up),
        like(w_down),
    )
    scratch = (
        [pltpu.VMEM(a.shape, a.dtype) for a in results]
        + [pltpu.VMEM(arrays[i].shape, arrays[i].dtype) for i in (0, 1, 2, 3, 7, 8, 9)]
        + legs(feats, 6)
        + [pltpu.VMEM((2, NX, rows, feats), BF)] * 2
        + [pltpu.VMEM((2,) + a.shape[1:], BF) for a in (w_gate, w_up, w_down)]
        + [pltpu.VMEM((NX, rows, feats), BF)] * 2
        + [pltpu.VMEM((16, rows), BF), pltpu.VMEM((NX, 16, rows), BF)]
        + [pltpu.VMEM((rows, 3 * hid), BF), pltpu.VMEM((2, rows, 3 * hid), BF)]
        + legs(feats + LANES, 4)
        + [
            pltpu.VMEM((feats, feats), BF),
            pltpu.VMEM((2, 2 * toks, half), BF),
            pltpu.VMEM((2, NX, 2 * toks, half), BF),
            pltpu.VMEM((n, n, FIRST, 16, LANES), BF),
            pltpu.VMEM((n, n, TILES - FIRST, 16, LANES), BF),
            pltpu.VMEM((2 * toks, TILES * LANES), F32),
            pltpu.VMEM((2 * toks, TILES * LANES), F32),
            pltpu.VMEM((NX, 2 * toks, half), BF),
            pltpu.VMEM((NX, 2 * toks, half), BF),
            pltpu.VMEM((toks, half), BF),
            pltpu.VMEM((toks, half), BF),
            pltpu.VMEM((32768, LANES), BF),
            pltpu.SemaphoreType.DMA((1,)),
            pltpu.SemaphoreType.DMA((76,)),
            pltpu.SemaphoreType.DMA((len(arrays) + len(results),)),
        ]
    )
    made = pl.pallas_call(
        functools.partial(kernel, n),
        out_shape=results,
        in_specs=[hbm] * len(arrays),
        out_specs=(hbm,) * len(results),
        scratch_shapes=scratch,
        compiler_params=pltpu.CompilerParams(
            collective_id=0, has_side_effects=True, vmem_limit_bytes=LIMIT
        ),
    )(*arrays)
    given = pl.pallas_call(
        hand_out,
        out_shape=results,
        in_specs=[hbm] * len(results),
        out_specs=(hbm,) * len(results),
        scratch_shapes=[pltpu.VMEM(a.shape, a.dtype) for a in results]
        + [pltpu.SemaphoreType.DMA((len(results),))] * 2,
        compiler_params=pltpu.CompilerParams(vmem_limit_bytes=LIMIT),
    )(*made)
    return (given[0], given[1].T) + tuple(given[2:])


def solution(mesh):
    placed = (
        P("ep", "tp"),
        P("ep", "tp"),
        P("ep", None),
        P("ep", None),
        P("ep", None, "tp"),
        P("ep", None, "tp"),
        P("ep", "tp", None),
        P("ep", "tp"),
        P("ep", "tp"),
        P("tp", "ep"),
    )
    return jax.shard_map(
        body,
        mesh=mesh,
        in_specs=placed,
        out_specs=(
            P("ep", "tp"),
            P("ep", None),
            P("ep", None, "tp"),
            P("ep", None, "tp"),
            P("ep", "tp", None),
        ),
        check_vma=False,
    )
```

```python
import functools
import math

import jax
import jax.numpy as jnp
from jax import lax
from jax.experimental import pallas as pl
from jax.experimental.pallas import tpu as pltpu
from jax.sharding import PartitionSpec as P

MESH = pl.DeviceIdType.MESH
BF = jnp.bfloat16
F32 = jnp.float32
NX = 4
LIMIT = 60 * 1024 * 1024
LANES = 128
TILES = 9
FIRST = 5


def dot(a, b, ca, cb, **kw):
    return lax.dot_general(a, b, (((ca,), (cb,)), ((), ())), preferred_element_type=F32, **kw)


def iota(shape, dim):
    return lax.broadcasted_iota(jnp.int32, shape, dim)


def one_hot(cond):
    return jnp.where(cond, 1.0, 0.0).astype(BF)


def kernel(
    n,
    tok_hbm, dy_hbm, gw_hbm, ids_hbm, wg_hbm, wu_hbm, wd_hbm, sg_hbm, su_hbm, sd_hbm,
    gt_hbm, gg_hbm, ggrad_hbm, ugrad_hbm, dgrad_hbm,
    gt_ref, gg_ref, ggrad, ugrad, dgrad, tok_ref, dy_ref, gw_ref, ids_ref, sg_ref, su_ref, sd_ref,
    pack_a, pack_b, buf_a, buf_b, mid_a, mid_b, rx, rd, wg, wu, wd,
    rs_out, rs_in, rr_out, rr_in, dd_out, dd, ret_out, ret_1, ret_mid, ret_2,
    sel, s_out, sx, g1, g2, pre_out, pre_in, piece_out, piece_in, fx_out, fx_in, tally,
    ssem, rsem, lsem,
):
    toks, feats = tok_ref.shape
    hid = wg_hbm.shape[2]
    rows = 2 * n * n
    msg = 2 * n
    half = feats // 2
    shared = sg_ref.shape[1]
    top = ids_ref.shape[0]
    edges = sorted({0, min(3, n), min(5, n), n})
    chunks = list(zip(edges, edges[1:]))
    near = sorted({0, 1, min(3, n), min(5, n), n})
    near_chunks = list(zip(near, near[1:]))

    ep = lax.axis_index("ep")
    x = lax.axis_index("tp")
    c = lax.rem(ep, 2)
    y = lax.rem(ep // 2, n)
    z = ep // (2 * n)
    sib = (ep + 1 - 2 * c, x)

    def away(p):
        return (p % 2) * ((p + 1) // 2) + (1 - p % 2) * ((n - p // 2) % n)

    def at_y(k):
        return ((z * n + lax.rem(y + k, n)) * 2 + c, x)

    def at_z(k):
        return ((lax.rem(z + k, n) * n + y) * 2 + c, x)

    def at_x(k):
        return (ep, lax.rem(x + k, NX))

    pending = []
    taken = [0]
    sent = [0]

    class Arrival:
        def __init__(self, ref):
            self.ref, self.sem = ref, taken[0]
            taken[0] += 1
            assert self.sem < rsem.shape[0]

        def wait(self):
            pltpu.make_async_copy(self.ref, self.ref, rsem.at[self.sem]).wait()
            pending.remove(self)

    class Local:
        def __init__(self, src, dst, sem):
            self.made = pltpu.make_async_copy(src, dst, lsem.at[sem])

        def start(self):
            self.made.start()
            pending.append(self)

        def wait(self):
            self.made.wait()
            pending.remove(self)

    def size(ref):
        return math.prod(ref.shape) * ref.dtype.itemsize

    def send(src, dst, arrival, to, times=1):
        pltpu.make_async_remote_copy(
            src_ref=src, dst_ref=dst, send_sem=ssem.at[0], recv_sem=rsem.at[arrival.sem],
            device_id=to, device_id_type=MESH,
        ).start()
        sent[0] += times * size(src)
        if arrival not in pending:
            pending.append(arrival)

    def send_each(low, high, arrival, make):
        if low < high:

            def step(i, carry):
                src, dst, to = make(low + high - 1 - i)
                send(src, dst, arrival, to, high - low)
                return carry

            lax.fori_loop(low, high, step, 0)

    def finish():
        for one in list(pending):
            one.wait()
        span = tally.at[pl.ds(0, sent[0] // 256)]
        pltpu.make_async_copy(span, span, ssem.at[0]).wait()

    moves = (
        (ids_hbm, ids_ref), (gw_hbm, gw_ref), (tok_hbm, tok_ref), (dy_hbm, dy_ref),
        (sg_hbm, sg_ref), (su_hbm, su_ref), (sd_hbm, sd_ref),
        (wg_hbm.at[0], wg.at[c]), (wu_hbm.at[0], wu.at[c]), (wd_hbm.at[0], wd.at[c]),
    )
    loads = [Local(a, b, i) for i, (a, b) in enumerate(moves)]
    for load in loads[:4]:
        load.start()

    barrier = pltpu.get_barrier_semaphore()
    for p in reversed(range(1, n)):
        for to in (at_y(away(p)), at_z(away(p))):
            pl.semaphore_signal(barrier, inc=1, device_id=to, device_id_type=MESH)
    for k in reversed(range(NX)):
        if k:
            pl.semaphore_signal(barrier, inc=1, device_id=at_x(k), device_id_type=MESH)
        pl.semaphore_signal(
            barrier, inc=1, device_id=(sib[0], lax.rem(x + k, NX)), device_id_type=MESH
        )
    for load in loads[4:]:
        load.start()
    for load in loads[:4]:
        load.wait()

    ids = ids_ref[...]
    gates = gw_ref[...].astype(F32)
    row = iota((rows, toks), 0)
    slot = row % 2
    outer, inner = away(row // msg), away((row // 2) % n)
    earlier = one_hot(iota((toks, toks), 0) < iota((toks, toks), 1))

    def place(expert):
        named = [ids[k : k + 1] == expert for k in range(top)]
        hits = functools.reduce(jnp.logical_or, named)
        before = dot(one_hot(hits), earlier, 1, 0)
        return named, jnp.logical_and(hits, before == slot.astype(F32))

    named_a, here_a = place(((z + outer) % n) * n + (y + inner) % n)
    named_b, here_b = place(((z + inner) % n) * n + (y + outer) % n)
    weight_b = sum(jnp.where(named_b[k], gates[k : k + 1], 0.0) for k in range(top))
    put_a = one_hot(here_a)
    put_b = jnp.where(here_b, weight_b, 0.0).astype(BF)
    tok = tok_ref[...]
    dy = dy_ref[...]
    pack_a[...] = dot(put_a, tok, 1, 0).astype(BF).reshape(n, msg, feats)
    pack_b[...] = dot(put_b, dy, 1, 0).astype(BF).reshape(n, msg, feats)

    pl.semaphore_wait(barrier, 2 * (n - 1) + 2 * NX - 1)

    others = pl.ds(1, n - 1)
    a1 = Arrival(buf_a.at[others])
    b1 = Arrival(buf_b.at[others])
    send_each(1, n, a1, lambda p: (pack_a.at[p], buf_a.at[p], at_z(away(p))))
    send_each(1, n, b1, lambda p: (pack_b.at[p], buf_b.at[p], at_y(away(p))))

    for load in loads[4:7]:
        load.wait()
    tiles = []
    for block in (sg_ref[...], su_ref[...], sd_ref[...]):
        pad = jnp.zeros((16, TILES // 3 * LANES - shared), BF)
        block = jnp.concatenate([block, pad], axis=1)
        tiles += [block[:, i * LANES : (i + 1) * LANES] for i in range(TILES // 3)]
    for i, tile in enumerate(tiles):
        if i < FIRST:
            g1[y, z, i] = tile
        else:
            g2[z, y, i - FIRST] = tile
    w1 = Arrival(g1.at[0, pl.ds(0, n - 1)])
    w2 = Arrival(g2.at[0, pl.ds(0, n - 1)])

    def send_weights():
        send_each(1, n, w1, lambda p: (g1.at[y, z], g1.at[y, z], at_z(away(p))))
        send_each(1, n, w2, lambda p: (g2.at[z, y], g2.at[z, y], at_y(away(p))))

    send_weights()

    col = iota((feats, feats), 1)
    col_in = col % half
    feature = 32 * (col_in // 16) + 16 * (col // half) + col_in % 16
    sel[...] = one_hot(iota((feats, feats), 0) == feature)
    s_all = dot(jnp.concatenate([tok, dy], axis=0), sel[...], 1, 0).astype(BF)
    s_out[0] = s_all[:, :half]
    s_out[1] = s_all[:, half:]
    sx[c, x] = s_out[c]
    s_same = Arrival(sx.at[0, pl.ds(0, NX - 1)])
    s_other = Arrival(sx.at[0])
    send_each(1, NX, s_same, lambda k: (s_out.at[c], sx.at[c, x], at_x(k)))
    send_each(0, NX, s_other, lambda k: (
        s_out.at[1 - c], sx.at[c, x], (sib[0], lax.rem(x + k, NX))))

    w_sib = []
    for load, ref in zip(loads[7:], (wg, wu, wd)):
        load.wait()
        w_sib.append(Arrival(ref.at[0]))
        send(ref.at[c], ref.at[c], w_sib[-1], sib)

    turned_row = iota((rows, rows), 0)
    turned = ((turned_row // 2) % n) * msg + (turned_row // msg) * 2 + turned_row % 2
    turn_f32 = jnp.where(iota((rows, rows), 1) == turned, 1.0, 0.0)
    turn = turn_f32.astype(BF)
    buf_a[0] = pack_a[0]
    buf_b[0] = pack_b[0]

    def part(p):
        return pl.ds(pl.multiple_of(p * msg, msg), msg)

    def spans_of(pairs):
        return [pl.ds(low * msg, (high - low) * msg) for low, high in pairs]

    spans, near_spans = spans_of(chunks), spans_of(near_chunks)
    a1.wait()
    mid_a[...] = dot(turn, buf_a[...].reshape(rows, feats), 1, 0).astype(BF).reshape(n, msg, feats)
    a2 = [
        Arrival(mid_a.at[pl.ds(max(low, 1), high - max(low, 1))]) if high > 1 else None
        for low, high in near_chunks
    ]
    for (low, high), arrival in zip(near_chunks, a2):
        send_each(max(low, 1), high, arrival, lambda p: (
            mid_a.at[p], rx.at[c, x, part(p)], at_y(away(p))))
    rx[c, x, 0:msg] = mid_a[0]
    b1.wait()
    mid_b[...] = dot(turn, buf_b[...].reshape(rows, feats), 1, 0).astype(BF).reshape(n, msg, feats)
    b2 = [
        Arrival(mid_b.at[pl.ds(max(low, 1), high - max(low, 1))]) if high > 1 else None
        for low, high in near_chunks
    ]
    for (low, high), arrival in zip(near_chunks, b2):
        send_each(max(low, 1), high, arrival, lambda p: (
            mid_b.at[p], rd.at[c, x, part(p)], at_z(away(p))))
    rd[c, x, 0:msg] = mid_b[0]

    class Ring:
        def __init__(self, buf, pos, go):
            self.buf, self.pos, self.go, self.step = buf, pos, go, 0
            self.flying = []

        def block(self, k):
            return lax.rem(self.pos + k + 2 * n, n)

        def forward(self):
            for arrival in self.flying:
                arrival.wait()
            self.flying = []
            s, last = self.step, n // 2 - 1
            if s <= last:
                if s < last:
                    arrival = Arrival(self.buf.at[pl.ds(0, 2)])
                else:
                    arrival = Arrival(self.buf.at[0])
                self.flying.append(arrival)
                for way in (1, -1):
                    at = self.buf.at[self.block(-way * s)]
                    if s == last:
                        at = at.at[pl.ds(0, n // 2) if way == 1 else pl.ds(n // 2, n // 2)]
                    send(at, at, arrival, self.go(way % n))
            self.step += 1

    ring1 = Ring(g1, y, at_y)
    ring2 = Ring(g2, z, at_z)

    def rings():
        ring1.forward()
        ring2.forward()

    def rings_first():
        w1.wait()
        ring1.forward()
        w2.wait()
        ring2.forward()

    left, right = lax.rem(x + NX - 1, NX), lax.rem(x + 1, NX)

    def to_x(buf, at, h, k):
        ref = buf.at[c, at, near_spans[h]]
        arrival = Arrival(ref)
        send(ref, ref, arrival, at_x(k % NX))
        return arrival

    x_right, x_left, d_right, d_left = [], [], [], []
    for h in range(len(near_chunks)):
        if a2[h]:
            a2[h].wait()
        x_right.append(to_x(rx, x, h, 1))
        if b2[h]:
            b2[h].wait()
        d_left.append(to_x(rd, x, h, -1))
        x_left.append(to_x(rx, x, h, -1))
        d_right.append(to_x(rd, x, h, 1))
        if h == 1:
            rings_first()

    x_on, d_on = [], []
    for h in range(len(near_chunks)):
        x_right[h].wait()
        x_on.append(to_x(rx, left, h, 1))
        d_left[h].wait()
        d_on.append(to_x(rd, right, h, -1))
        if h == 2:
            rings()

    for arrival in w_sib:
        arrival.wait()

    def at_quarter(q):
        return pl.ds(pl.multiple_of(q * feats, feats), feats)

    def w_quarter(q):
        return jnp.concatenate(
            [ref[u, at_quarter(q)] for ref in (wg, wu) for u in range(2)], axis=1
        )

    def down_quarter(q):
        return jnp.concatenate([wd[u, :, at_quarter(q)] for u in range(2)], axis=0)

    both = 2 * hid
    pre = jnp.zeros((rows, 2 * both), F32)
    q_back = jnp.zeros((rows, both), F32)
    for k in (0, 1, 3, 2):
        if k == 1:
            for arrival in x_left:
                arrival.wait()
        if k == 3:
            for arrival in d_right:
                arrival.wait()
        if k == 2:
            for arrival in x_on + d_on:
                arrival.wait()
        q = lax.rem(x + k, NX)
        pre = pre + dot(rx[c, q], w_quarter(q), 1, 0)
        q_back = q_back + dot(rd[c, q], down_quarter(q), 1, 1)
    q_back = dot(turn_f32, q_back, 1, 0, precision=lax.Precision.HIGHEST)

    def silu_parts(pre_gate, pre_up, back):
        sigma = jax.nn.sigmoid(pre_gate)
        active = pre_gate * sigma
        d_gate = back * pre_up * sigma * (1.0 + pre_gate * (1.0 - sigma))
        return active * pre_up, jnp.concatenate([d_gate, back * active], axis=1).astype(BF)

    hidden, d_both = silu_parts(pre[:, :both], pre[:, both:], q_back)
    router = jnp.sum(hidden * q_back, axis=1, keepdims=True)

    def coded(value, at):
        first = value.astype(BF).astype(F32)
        return jnp.where(at == 0, first, jnp.where(at == 1, value - first, 0.0)).astype(BF)

    def as_row(column):
        return jnp.broadcast_to(column, (rows, 16)).T

    def row_sum(tile):
        return jnp.sum(tile.astype(F32), axis=0, keepdims=True)

    tile_row = iota((16, rows), 0)
    rr_out[...] = coded(as_row(router), tile_row)
    router_rs = Arrival(rr_in.at[pl.ds(1, NX - 1)])
    send_each(1, NX, router_rs, lambda k: (rr_out, rr_in.at[k], at_x(k)))
    for k in (2, 1, 3, 0):
        rs_out[k] = dot(d_both, w_quarter(lax.rem(x + k, NX)), 1, 1).astype(BF)
    rs = {}
    for h in reversed(range(len(chunks))):
        rs[h] = Arrival(rs_in.at[pl.ds(1, NX - 1), spans[h]])
        for k in (2, 1, 3):
            send(rs_out.at[k, spans[h]], rs_in.at[k, spans[h]], rs[h], at_x(k))
    rings()

    first_half = c == 0
    hidden = dot(turn, hidden.astype(BF), 1, 0).astype(BF)
    parts = [
        jnp.concatenate(
            [a[:, u * hid : (u + 1) * hid] for a in (d_both[:, :both], d_both[:, both:], hidden)],
            axis=1,
        )
        for u in range(2)
    ]
    dd[c] = jnp.where(first_half, parts[0], parts[1])
    dd_out[...] = jnp.where(first_half, parts[1], parts[0])
    dd_sib, x_sib, d_sib = Arrival(dd.at[0]), Arrival(rx.at[0]), Arrival(rd.at[0])
    send(dd_out, dd.at[c], dd_sib, sib)
    send(rx.at[c], rx.at[c], x_sib, sib)
    send(rd.at[c], rd.at[c], d_sib, sib)
    stores = [
        Local(a, b, len(loads) + i)
        for i, (a, b) in enumerate((
            (gt_ref, gt_hbm), (gg_ref, gg_hbm),
            (ggrad, ggrad_hbm), (ugrad, ugrad_hbm), (dgrad, dgrad_hbm),
        ))
    ]

    def weight_gradients():
        for arrival in (dd_sib, x_sib, d_sib):
            arrival.wait()
        parts = jnp.concatenate([dd[0], dd[1]], axis=0)
        for q in range(NX):
            span = slice(q * feats, (q + 1) * feats)
            rows_x = jnp.concatenate([rx[0, q], rx[1, q]], axis=0)
            rows_d = jnp.concatenate([rd[0, q], rd[1, q]], axis=0)
            grads = dot(rows_x, parts[:, : 2 * hid], 0, 0).astype(BF)
            ggrad[0, span] = grads[:, :hid]
            ugrad[0, span] = grads[:, hid:]
            dgrad[0, :, span] = dot(parts[:, 2 * hid :], rows_d, 0, 0).astype(BF)
        for store in stores[2:]:
            store.start()


    router_rs.wait()
    r_all = row_sum(rr_out[...])
    for k in range(1, NX):
        r_all = r_all + row_sum(rr_in[k])
    r_total = coded(jnp.broadcast_to(r_all, (LANES, rows)).T, iota((rows, LANES), 1))
    back_1 = Arrival(ret_1.at[others])
    for h in reversed(range(len(chunks))):
        low, high = chunks[h]
        rs[h].wait()
        total = rs_out[0, spans[h]].astype(F32)
        for k in range(1, NX):
            total = total + rs_in[k, spans[h]].astype(F32)
        r_part = r_total[low * msg : high * msg]
        block = jnp.concatenate([total.astype(BF), r_part], axis=1)
        ret_out[low:high] = block.reshape(high - low, msg, feats + LANES)
        send_each(max(low, 1), high, back_1, lambda p: (
            ret_out.at[p], ret_1.at[p], at_y(n - away(p))))
    ret_1[0] = ret_out[0]
    weight_gradients()
    rings()

    def weights(i):
        if i < FIRST:
            parts = [g1[:, k, i].reshape(n * 16, LANES) for k in range(n)]
        else:
            parts = [g2[k, :, i - FIRST].reshape(n * 16, LANES) for k in range(n)]
        return jnp.concatenate(parts, axis=0)

    def matrix(m):
        return jnp.concatenate([weights(3 * m + i) for i in range(3)], axis=1)

    def features(low):
        return jnp.concatenate(
            [
                jnp.concatenate([sx[s, q, low : low + toks] for q in range(NX)], axis=1)
                for s in range(2)
            ],
            axis=0,
        )

    width = 3 * LANES

    def shared_one():
        s_same.wait()
        s_other.wait()
        s_tok = features(0)
        pre_out[:, :width] = dot(s_tok, matrix(0), 1, 0)
        pre_out[:, width : 2 * width] = dot(s_tok, matrix(1), 1, 0)
        pre_out[:, 2 * width :] = dot(features(toks), matrix(2), 1, 0)
        arrival = Arrival(pre_in)
        send(pre_out, pre_in, arrival, sib)
        return arrival


    back_1.wait()
    wide = feats + LANES
    ret_mid[...] = dot(turn, ret_1[...].reshape(rows, wide), 1, 0).astype(BF).reshape(n, msg, wide)
    back_2 = Arrival(ret_2.at[others])
    send_each(1, n, back_2, lambda p: (ret_mid.at[p], ret_2.at[p], at_z(n - away(p))))
    ret_2[0] = ret_mid[0]
    rings()
    pre_sib = shared_one()

    pre_sib.wait()
    s_pre = pre_out[...] + pre_in[...]
    _, s_both = silu_parts(s_pre[:, :width], s_pre[:, width : 2 * width], s_pre[:, 2 * width :])
    piece = dot(s_both[:, :width], matrix(0), 1, 1) + dot(s_both[:, width:], matrix(1), 1, 1)
    for q in range(NX):
        piece_out[q] = piece[:, q * half : (q + 1) * half].astype(BF)
    s_rs = Arrival(piece_in.at[pl.ds(1, NX - 1)])
    send_each(1, NX, s_rs, lambda k: (
        piece_out.at[lax.rem(x + k, NX)], piece_in.at[k], at_x(k)))
    s_rs.wait()
    s_sum = piece_out[x].astype(F32)
    for k in range(1, NX):
        s_sum = s_sum + piece_in[k].astype(F32)
    s_sum = s_sum.astype(BF)
    s_own = jnp.where(first_half, s_sum[:toks], s_sum[toks:])
    fx_out[...] = jnp.where(first_half, s_sum[toks:], s_sum[:toks])
    s_fx = Arrival(fx_in)
    send(fx_out, fx_in, s_fx, sib)

    back_2.wait()
    came = ret_2[...].reshape(rows, wide)
    routed = dot(put_a, came[:, :feats], 0, 0)
    routers = jnp.sum(came[:, feats:].astype(F32), axis=1, keepdims=True)
    gg_ref[...] = jnp.concatenate(
        [
            jnp.sum(
                jnp.where(jnp.logical_and(here_a, named_a[k]), routers, 0.0),
                axis=0, keepdims=True,
            )
            for k in range(top)
        ],
        axis=0,
    ) / gates
    stores[1].start()
    s_fx.wait()
    s_other_half = fx_in[...]
    s_both = jnp.concatenate(
        [
            jnp.where(first_half, s_own, s_other_half),
            jnp.where(first_half, s_other_half, s_own),
        ],
        axis=1,
    )
    gt_ref[...] = (routed + dot(s_both, sel[...], 1, 1)).astype(BF)
    stores[0].start()
    finish()


def hand_out(*refs):
    count = (len(refs) - 2) // 3
    ins, outs, held = refs[:count], refs[count : 2 * count], refs[2 * count : 3 * count]
    fetch, store = refs[3 * count :]
    reads = [pltpu.make_async_copy(ins[i], held[i], fetch.at[i]) for i in range(count)]
    writes = [pltpu.make_async_copy(held[i], outs[i], store.at[i]) for i in range(count)]
    for read in reads:
        read.start()
    for read, write in zip(reads, writes):
        read.wait()
        write.start()
    for write in writes:
        write.wait()


def body(tokens, out_grad, gate_weights, expert_ids, w_gate, w_up, w_down, s_gate, s_up, s_down):
    n = round((lax.axis_size("ep") // 2) ** 0.5)
    toks, feats = tokens.shape
    hid = w_gate.shape[2]
    rows, msg, half = 2 * n * n, 2 * n, feats // 2
    vmem = pl.BlockSpec(memory_space=pltpu.VMEM)
    hbm = pl.BlockSpec(memory_space=pltpu.HBM)

    def legs(lanes, count):
        return [pltpu.VMEM((n, msg, lanes), BF) for _ in range(count)]

    def like(a):
        return jax.ShapeDtypeStruct(a.shape, a.dtype)

    arrays = (
        tokens, out_grad, gate_weights.T, expert_ids.T, w_gate, w_up, w_down,
        s_gate, s_up, s_down.T,
    )
    results = (
        like(tokens),
        jax.ShapeDtypeStruct(gate_weights.shape[::-1], F32),
        like(w_gate),
        like(w_up),
        like(w_down),
    )
    scratch = (
        [pltpu.VMEM(a.shape, a.dtype) for a in results]
        + [pltpu.VMEM(arrays[i].shape, arrays[i].dtype) for i in (0, 1, 2, 3, 7, 8, 9)]
        + legs(feats, 6)
        + [pltpu.VMEM((2, NX, rows, feats), BF)] * 2
        + [pltpu.VMEM((2,) + a.shape[1:], BF) for a in (w_gate, w_up, w_down)]
        + [pltpu.VMEM((NX, rows, feats), BF)] * 2
        + [pltpu.VMEM((16, rows), BF), pltpu.VMEM((NX, 16, rows), BF)]
        + [pltpu.VMEM((rows, 3 * hid), BF), pltpu.VMEM((2, rows, 3 * hid), BF)]
        + legs(feats + LANES, 4)
        + [
            pltpu.VMEM((feats, feats), BF),
            pltpu.VMEM((2, 2 * toks, half), BF),
            pltpu.VMEM((2, NX, 2 * toks, half), BF),
            pltpu.VMEM((n, n, FIRST, 16, LANES), BF),
            pltpu.VMEM((n, n, TILES - FIRST, 16, LANES), BF),
            pltpu.VMEM((2 * toks, TILES * LANES), F32),
            pltpu.VMEM((2 * toks, TILES * LANES), F32),
            pltpu.VMEM((NX, 2 * toks, half), BF),
            pltpu.VMEM((NX, 2 * toks, half), BF),
            pltpu.VMEM((toks, half), BF),
            pltpu.VMEM((toks, half), BF),
            pltpu.VMEM((32768, LANES), BF),
            pltpu.SemaphoreType.DMA((1,)),
            pltpu.SemaphoreType.DMA((76,)),
            pltpu.SemaphoreType.DMA((len(arrays) + len(results),)),
        ]
    )
    made = pl.pallas_call(
        functools.partial(kernel, n),
        out_shape=results,
        in_specs=[hbm] * len(arrays),
        out_specs=(hbm,) * len(results),
        scratch_shapes=scratch,
        compiler_params=pltpu.CompilerParams(
            collective_id=0, has_side_effects=True, vmem_limit_bytes=LIMIT
        ),
    )(*arrays)
    given = pl.pallas_call(
        hand_out,
        out_shape=results,
        in_specs=[hbm] * len(results),
        out_specs=(hbm,) * len(results),
        scratch_shapes=[pltpu.VMEM(a.shape, a.dtype) for a in results]
        + [pltpu.SemaphoreType.DMA((len(results),))] * 2,
        compiler_params=pltpu.CompilerParams(vmem_limit_bytes=LIMIT),
    )(*made)
    return (given[0], given[1].T) + tuple(given[2:])


def solution(mesh):
    placed = (
        P("ep", "tp"),
        P("ep", "tp"),
        P("ep", None),
        P("ep", None),
        P("ep", None, "tp"),
        P("ep", None, "tp"),
        P("ep", "tp", None),
        P("ep", "tp"),
        P("ep", "tp"),
        P("tp", "ep"),
    )
    return jax.shard_map(
        body,
        mesh=mesh,
        in_specs=placed,
        out_specs=(
            P("ep", "tp"),
            P("ep", None),
            P("ep", None, "tp"),
            P("ep", None, "tp"),
            P("ep", "tp", None),
        ),
        check_vma=False,
    )
```
